512 devices in a mesh: graph: 128 (over z, x, core), mp: 4 (over y).
Axes of the slice: x: 4, y: 4, z: 16, core: 2. Of those that a mesh axis runs over, the one named last changes fastest.
Arguments:
- agents: float32 [32768, 256], P('graph'), may hold values from -30 to 30
- latents: float32 [64, 256], P(None, 'mp'), may hold values from -40 to 40
- w_local: float32 [256, 256], P(None, 'mp'), may hold values from -0.375 to 0.375
- w_value: float32 [256, 256], P(None, 'mp'), may hold values from -0.375 to 0.375
- w_up: float32 [256, 512], P(None, 'mp'), may hold values from -0.375 to 0.375
- w_down: float32 [512, 256], P('mp'), may hold values from -0.25 to 0.25
- neighbours: int32 [32768, 16], P('graph'), may hold values from 0 to 2303
- degree: int32 [32768], P('graph'), may hold values from 1 to 16
- send_rows: int32 [128, 128, 16], P('graph'), may hold values from 0 to 255
- cotangent: float32 [32768, 256], P('graph'), may hold values from -6 to 6
Outputs:
- updated: float32 [32768, 256], P('graph', 'mp')
- grad_agents: float32 [32768, 256], P('graph', 'mp')
- grad_latents: float32 [64, 256], P(None, 'mp')
- grad_local: float32 [256, 256], P(None, 'mp')
- grad_value: float32 [256, 256], P(None, 'mp')
- grad_up: float32 [256, 512], P(None, 'mp')
- grad_down: float32 [512, 256], P('mp')
The draws below stay inside these ranges and needn't reach their ends.
All inputs are finite; a program needn't handle non-finite values.
Results may differ from the reference program's by a relative error of at most 0.0003.
Values sent between devices are 32-bit elements; how exact they have to be, the bound alone decides.
A program may use at most 64 MiB of HBM per device.

```python
import math
import jax
import jax.numpy as jnp
from jax import lax

D = 256
FF = 512
HEADS = 4
HEAD_DIM = 64
VNODES = 64
NBR = 16
SLOTS = 16
A_DEV = 256
AGENTS = 32768
N_GRAPH = 128


def draw_agents(key, part):
    folded = jax.random.fold_in(key, 11)
    k_main, k_row, k_col = jax.random.split(folded, 3)
    position = jnp.arange(AGENTS, dtype=jnp.float32) / AGENTS
    entries = jnp.clip(jax.random.normal(k_main, (AGENTS, D), jnp.float32), -4.0, 4.0)
    ramp_up = 3.0 ** position
    row_scale = jnp.exp(jax.random.uniform(k_row, (AGENTS, 1), jnp.float32, math.log(0.4), math.log(1.3)))
    offset = jax.random.uniform(k_col, (1, D), jnp.float32, -1.0, 1.0)
    result = offset + ramp_up[:, None] * row_scale * entries
    return result


def draw_latents(key, part):
    folded = jax.random.fold_in(key, 23)
    result = jnp.clip(jax.random.normal(folded, (VNODES, D), jnp.float32), -4.0, 4.0)
    return result


def touch_ends(drawn, own_key, least, high):
    index_at = [jax.random.randint(jax.random.fold_in(own_key, axis), (), 0, length) for axis, length in enumerate(drawn.shape)]
    main_axis = drawn.shape.index(max(drawn.shape))
    beside = index_at[:main_axis] + [(index_at[main_axis] + 1) % drawn.shape[main_axis]] + index_at[main_axis + 1:]
    return drawn.at[tuple(index_at)].set(least).at[tuple(beside)].set(high)


def level_of(key, dims, cuts, least, high):
    factor_of = 1.0
    for dim, shards_of in cuts:
        heights = jax.random.uniform(jax.random.fold_in(jax.random.fold_in(key, 6), dim), (shards_of,), jnp.float32, least / len(cuts), high / len(cuts))
        factor_of = factor_of * jnp.repeat(jnp.exp(heights), dims[dim] // shards_of).reshape((-1,) + (1,) * (len(dims) - 1 - dim))
    return factor_of


def bell_draw(key, dims, spread, most, pieces=(), kind=jnp.bfloat16):
    values = spread * jax.random.normal(key, dims, jnp.float32)
    if pieces:
        values = values * level_of(key, dims, pieces, -0.22, 0.18)
    return jnp.clip(values, -most, most).astype(kind)


def setup_inputs(seed: int = 0) -> dict:
    key_list = jax.random.split(jax.random.key(seed), 11)
    agents = draw_agents(jax.random.fold_in(key_list[10], 71), 0)
    latents = draw_latents(jax.random.fold_in(key_list[10], 71), 0)
    w_local = bell_draw(key_list[2], (D, D), D ** -0.5, 0.375, ((1, 4),), jnp.float32)
    w_value = bell_draw(key_list[3], (D, D), D ** -0.5, 0.375, ((1, 4),), jnp.float32)
    w_up = bell_draw(key_list[4], (D, FF), D ** -0.5, 0.375, ((1, 4),), jnp.float32)
    w_down = bell_draw(key_list[5], (FF, D), FF ** -0.5, 0.25, ((0, 4),), jnp.float32)
    neighbours = touch_ends(jax.random.randint(key_list[6], (AGENTS, NBR), 0, A_DEV + N_GRAPH * SLOTS), jax.random.fold_in(key_list[6], 1), 0, (A_DEV + N_GRAPH * SLOTS) - 1).astype(jnp.int32)
    degree = touch_ends(jax.random.randint(key_list[7], (AGENTS,), 1, NBR + 1), jax.random.fold_in(key_list[7], 1), 1, NBR).astype(jnp.int32)
    send_rows = touch_ends(jax.random.randint(key_list[8], (N_GRAPH, N_GRAPH, SLOTS), 0, A_DEV), jax.random.fold_in(key_list[8], 1), 0, A_DEV - 1).astype(jnp.int32)
    cotangent = bell_draw(key_list[9], (AGENTS, D), 1.0, 6.0, ((0, 128),), jnp.float32)
    return {"agents": agents, "latents": latents, "w_local": w_local, "w_value": w_value, "w_up": w_up, "w_down": w_down, "neighbours": neighbours, "degree": degree, "send_rows": send_rows, "cotangent": cotangent}


HIGHEST = lax.Precision.HIGHEST

def matmul(left, right):
    return jnp.dot(left, right, precision=HIGHEST, preferred_element_type=jnp.float32)

def layer(agents, latents, w_local, w_value, w_up, w_down, neighbours, degree, send_rows):
    proj_parts = matmul(agents, w_local).reshape(N_GRAPH, A_DEV, D)
    values = matmul(agents, w_value)
    sources = jnp.arange(N_GRAPH, dtype=jnp.int32)
    nbr_parts = neighbours.reshape(N_GRAPH, A_DEV, NBR)
    degree_parts = degree.reshape(N_GRAPH, A_DEV)
    slot_ids = jnp.arange(NBR, dtype=jnp.int32)

    def partition_mean(part_index):
        received = proj_parts[sources[:, None], send_rows[:, part_index, :]]
        row_table = jnp.concatenate([proj_parts[part_index], received.reshape(N_GRAPH * SLOTS, D)], 0)
        gathered = row_table[nbr_parts[part_index]]
        own_degree = degree_parts[part_index]
        slot_mask = (slot_ids[None, :] < own_degree[:, None]).astype(jnp.float32)
        return lax.optimization_barrier(jnp.sum(gathered * slot_mask[:, :, None], 1)) / own_degree[:, None].astype(jnp.float32)
    message = lax.map(partition_mean, sources).reshape(AGENTS, D)
    score_scale = 1.0 / math.sqrt(HEAD_DIM)
    heads_x = agents.reshape(AGENTS, HEADS, HEAD_DIM)
    heads_q = latents.reshape(VNODES, HEADS, HEAD_DIM)
    heads_v = values.reshape(AGENTS, HEADS, HEAD_DIM)
    scores = jnp.einsum('mhe,ahe->mha', heads_q, heads_x, precision=HIGHEST) * score_scale
    prob = jax.nn.softmax(scores, axis=-1)
    attended = jnp.einsum('mha,ahe->mhe', prob, heads_v, precision=HIGHEST)
    fresh = latents + attended.reshape(VNODES, D)
    heads_f = fresh.reshape(VNODES, HEADS, HEAD_DIM)
    agent_scores = jnp.einsum('ahe,mhe->ahm', heads_x, heads_f, precision=HIGHEST) * score_scale
    agent_prob = jax.nn.softmax(agent_scores, axis=-1)
    readout = jnp.einsum('ahm,mhe->ahe', agent_prob, heads_f, precision=HIGHEST).reshape(AGENTS, D)
    hidden = agents + message + readout
    return hidden + matmul(jax.nn.silu(matmul(hidden, w_up)), w_down)

def reference(agents, latents, w_local, w_value, w_up, w_down, neighbours, degree, send_rows, cotangent):

    def forward(agent_in, latent_in, local_in, value_in, up_in, down_in):
        return layer(agent_in, latent_in, local_in, value_in, up_in, down_in, neighbours, degree, send_rows)
    updated, pullback = jax.vjp(forward, agents, latents, w_local, w_value, w_up, w_down)
    grads = pullback(cotangent)
    factor = 1.0 / math.sqrt(AGENTS)
    return (updated, grads[0], grads[1] * factor, grads[2] * factor, grads[3] * factor, grads[4] * factor, grads[5] * factor)
```

```python
import functools
import math
from types import SimpleNamespace

import jax
import jax.numpy as jnp
from jax import lax
from jax.experimental import pallas as pl
from jax.experimental.pallas import tpu as pltpu
from jax.sharding import PartitionSpec as P

HEAD = 64
VN = 64
SLOTS = 16
LANES = 128
MESH = pl.DeviceIdType.MESH
F32 = jnp.float32
BF16 = jnp.bfloat16


def dot(left, right, contract, precision):
    return lax.dot_general(
        left, right, (contract, ((), ())), precision=precision, preferred_element_type=F32
    )


def mm(left, right):
    return dot(left, right, ((1,), (0,)), lax.Precision.HIGHEST)


def mt(left, right):
    return dot(left, right, ((1,), (1,)), lax.Precision.HIGHEST)


def mb(left, right):
    return dot(left, right, ((1,), (0,)), lax.Precision.DEFAULT)


def mbt(left, right):
    return dot(left, right, ((1,), (1,)), lax.Precision.DEFAULT)


def split(x, axis):
    high = x.astype(BF16)
    low = (x - high.astype(F32)).astype(BF16)
    return jnp.concatenate([high, low], axis)


def halves(x):
    half = x.shape[0] // 2
    return x[:half] + x[half:]


def layer(nz, nxc, nmp, rows, dim, names, *refs):
    r = SimpleNamespace(**dict(zip(names, refs)))
    graph = lax.axis_index("graph")
    mp = lax.axis_index("mp")
    z = graph // nxc
    xc = lax.rem(graph, nxc)
    nb4 = nz // 4
    zb = z // 4
    zm = lax.rem(z, 4)
    ng = nz * nxc
    scale = 1.0 / math.sqrt(HEAD)
    factor = 1.0 / math.sqrt(rows * ng)

    def z_peer(d):
        return lax.rem(z + d, nz)

    def x_peer(d):
        return lax.rem(xc + d, nxc)

    def send(src, dst, ssem, rsem, device):
        pltpu.make_async_remote_copy(
            src_ref=src,
            dst_ref=dst,
            send_sem=ssem,
            recv_sem=rsem,
            device_id=device,
            device_id_type=MESH,
        ).start()

    def wait(ref, sem):
        pltpu.make_async_copy(ref, ref, sem).wait()

    def loop(low, high, body):
        def step(d, carry):
            body(d)
            return carry

        lax.fori_loop(low, high, step, 0)

    barrier = pltpu.get_barrier_semaphore()

    def greet(device):
        pl.semaphore_signal(barrier, inc=1, device_id=device, device_id_type=MESH)

    loop(1, nz, lambda d: greet({"graph": z_peer(d) * nxc + xc}))
    loop(1, nxc, lambda d: greet({"graph": z * nxc + x_peer(d)}))
    loop(1, nmp, lambda d: greet({"mp": lax.rem(mp + d, nmp)}))

    def group_start(give, got, sems):
        def go(d):
            peer = x_peer(d)
            send(give.at[peer], got.at[xc], sems.at[0], sems.at[1], {"graph": z * nxc + peer})

        loop(1, nxc, go)
        got[xc] = give[xc]

    def z_share(piece, got, sems):
        def go(d):
            send(piece, got.at[z], sems.at[2], sems.at[3], {"graph": z_peer(d) * nxc + xc})

        loop(1, nz, go)
        got[z] = piece[...]

    def group_gather(full, sems):
        def go(d):
            send(full.at[xc], full.at[xc], sems.at[4], sems.at[5], {"graph": z * nxc + x_peer(d)})

        loop(1, nxc, go)

    def wait_x(ref, sem):
        wait(ref.at[pl.ds(0, nxc - 1)], sem)

    def wait_z(ref, sem):
        wait(ref.at[pl.ds(0, nz - 1)], sem)

    def total(ref):
        acc = ref[0]
        for i in range(1, ref.shape[0]):
            acc = acc + ref[i]
        return acc

    def merged(ref):
        count = ref.shape[0]
        parts = [ref[i] for i in range(count)]
        tops = [part[:, 96:97] for part in parts]
        top = functools.reduce(jnp.maximum, tops)
        acc = parts[0] * jnp.exp(tops[0] - top)
        for i in range(1, count):
            acc = acc + parts[i] * jnp.exp(tops[i] - top)
        lane = lax.broadcasted_iota(jnp.int32, acc.shape, 1)
        return jnp.where(lane >= 96, top, acc)

    def rows_start(out, mid, zs, zr):
        for i in (0, 1, 3, 2)[: nb4] if nb4 != 2 else (0, 1):
            base = lax.rem(zb + nb4 - i, nb4) * 4
            for d in range(1 if i == 0 else 0, 4):
                peer = base + lax.rem(zm + d, 4)
                send(out.at[peer], mid.at[z], zs, zr.at[i], {"graph": peer * nxc + xc})
        mid[z] = out[z]

    def rows_forward(i, mid, land, zr, fs, fr):
        base = lax.rem(zb + i, nb4) * 4
        wait(mid.at[pl.ds(0, 3 if i == 0 else 4)], zr.at[i])

        def go(d):
            peer = x_peer(d)
            send(
                mid.at[pl.ds(base, 4), peer],
                land.at[pl.ds(base, 4), xc],
                fs,
                fr,
                {"graph": z * nxc + peer},
            )

        loop(1, nxc, go)
        land[pl.ds(base, 4), xc] = mid[pl.ds(base, 4), xc]

    def rows_wait(land, fr):
        wait(land.at[:, pl.ds(0, nxc - 1)], fr)

    def y_send(src_of, got, ssem, rsem):
        for d in range(1, nmp):
            peer = lax.rem(mp + d, nmp)
            send(src_of(peer), got.at[mp], ssem, rsem, {"mp": peer})

    def wait_y(ref, sem):
        wait(ref.at[pl.ds(0, nmp - 1)], sem)

    xt_all = r.agents[...].T
    r.xt[...] = xt_all.reshape(nmp, HEAD, rows)
    w_joined = jnp.concatenate([r.w_local[...], r.w_value[...]], 1)
    joined_t = mm(w_joined.T, xt_all)
    lt2 = split(joined_t[:HEAD], 0)
    r.lt2[...] = lt2
    r.vt[:HEAD] = joined_t[HEAD:]
    r.vt[HEAD:] = jnp.ones((HEAD, rows), F32)
    half = ng * 8
    chunk = 256
    for c in range(2 * half // chunk):
        cols = pl.ds(c * chunk, chunk)
        row_id = lax.broadcasted_iota(jnp.int32, (rows, chunk), 0)
        r.st[:, cols] = jnp.where(row_id == r.sends[:, cols], 1.0, 0.0).astype(BF16)
    rows_out = halves(mb(lt2, r.st[...]))
    packed = jnp.concatenate([rows_out[:, :half], rows_out[:, half:]], 0).T
    r.out1[...] = packed.reshape(nz, nxc, 8, LANES)
    pl.semaphore_wait(barrier, nz + nxc + nmp - 3)
    rows_start(r.out1, r.mid1, r.rsem.at[0], r.zsem1)

    xt = r.xt[mp]
    scores = mm(r.latents[...], xt) * scale
    local_top = jnp.max(scores, 1, keepdims=True)
    weights = jnp.exp(scores - local_top)
    r.weights[...] = weights
    part = mt(weights, r.vt[...])
    lane = lax.broadcasted_iota(jnp.int32, part.shape, 1)
    r.give1[...] = jnp.where(lane >= 96, local_top, part).reshape(r.give1.shape)
    group_start(r.give1, r.got1, r.s1)

    degree = r.degree[...].astype(F32)
    degree_col = jnp.broadcast_to(degree, (8, rows)).T[:, :1]
    slot = lax.broadcasted_iota(jnp.int32, (rows, SLOTS), 1)
    near = r.neighbours[...]
    far = near - rows
    k = far & 15
    far_col = rows + (k >> 3) * half + (far >> 4) * 8 + (k & 7)
    column = jnp.where(near < rows, near, far_col)
    r.nbm[...] = jnp.where(slot.astype(F32) < degree_col, column, -1)
    width = rows + 2 * half
    part_width = 768 if width % 768 == 0 else 256

    def count_rows(b):
        row = pl.multiple_of(b * 16, 16)
        nb = r.nbm[pl.ds(row, 16), :]
        for c in range(width // part_width):
            col = lax.broadcasted_iota(jnp.int32, (16, part_width), 1) + c * part_width
            acc = jnp.zeros((16, part_width), F32)
            for s in range(SLOTS):
                acc = acc + jnp.where(nb[:, s : s + 1] == col, 1.0, 0.0)
            r.counts[pl.ds(row, 16), pl.ds(c * part_width, part_width)] = acc.astype(BF16)

    def count_part(p):
        blocks = rows // 64
        loop(p * blocks, (p + 1) * blocks, count_rows)

    ct_all = r.cotangent[...].T
    r.ct[...] = ct_all.reshape(nmp, HEAD, rows)
    r.dact[...] = mm(r.w_down[...], ct_all)
    r.wut[...] = r.w_up[...].T
    r.wdt[...] = r.w_down[...].T

    wait_x(r.got1, r.s1.at[1])
    r.piece1[...] = merged(r.got1)
    z_share(r.piece1, r.gotz1, r.s1)
    rows_forward(0, r.mid1, r.land1, r.zsem1, r.rsem.at[1], r.rsem.at[2])
    count_part(0)
    wait_z(r.gotz1, r.s1.at[3])
    r.full1[xc] = merged(r.gotz1)
    group_gather(r.full1, r.s1)
    order = {1: (), 2: (1,), 4: (1, 3, 2)}[nb4]
    for p, i in enumerate(order):
        rows_forward(i, r.mid1, r.land1, r.zsem1, r.rsem.at[1], r.rsem.at[2])
        count_part(p + 1)
    for p in range(len(order) + 1, 4):
        count_part(p)

    wait_x(r.full1, r.s1.at[5])
    soft = r.full1[...].reshape(VN, LANES)
    inv_total = 1.0 / soft[:, 64:65]
    attended = soft[:, :HEAD] * inv_total
    r.attended[...] = attended
    r.weights[...] = r.weights[...] * (jnp.exp(local_top - soft[:, 96:97]) * inv_total)
    fresh = r.latents[...] + attended
    r.fresh[...] = fresh
    a_scores = mm(fresh, xt) * scale
    a_exp = jnp.exp(a_scores - jnp.max(a_scores, 0, keepdims=True))
    a_prob = a_exp / jnp.sum(a_exp, 0, keepdims=True)
    r.aprob[...] = a_prob
    r.fresh_t[...] = fresh.T
    readout = mm(r.fresh_t[...], a_prob)
    own = mbt(r.lt2[...], r.counts[:, pl.ds(0, rows)])

    def packed_product(left_low, left_high, land):
        both = split(land[...].reshape(half, LANES), 1)
        low = mb(left_low, both)
        high = mb(left_high, both)
        lane2 = lax.broadcasted_iota(jnp.int32, low.shape, 1) % LANES
        picked = jnp.where(lane2 < HEAD, low, high)
        return (picked[:, :LANES] + picked[:, LANES:]).T

    rows_wait(r.land1, r.rsem.at[2])
    far_sum = packed_product(
        r.counts[:, pl.ds(rows, half)], r.counts[:, pl.ds(rows + half, half)], r.land1
    )
    inv_degree = 1.0 / degree
    message = halves(own + far_sum) * inv_degree
    hidden = xt + message + readout
    r.hid[mp] = hidden
    y_send(lambda peer: r.hid.at[mp], r.hid, r.ysem.at[0], r.ysem.at[1])
    wait_y(r.hid, r.ysem.at[1])

    hid_all = r.hid[...].reshape(dim, rows)
    pre = mm(r.wut[...], hid_all)
    gate = 1.0 / (1.0 + jnp.exp(-pre))
    dpre = r.dact[...] * (gate * (1.0 + pre * (1.0 - gate)))
    r.dhp[...] = mm(r.w_up[...], dpre).reshape(r.dhp.shape)
    y_send(lambda peer: r.dhp.at[peer], r.rdh, r.ysem.at[2], r.ysem.at[3])
    act = pre * gate
    r.brp[...] = mm(r.wdt[...], act).reshape(r.brp.shape)
    y_send(lambda peer: r.brp.at[peer], r.rbr, r.ysem.at[4], r.ysem.at[5])
    r.rdh[mp] = r.dhp[mp] + r.ct[mp]
    r.rbr[mp] = r.brp[mp] + hidden
    wait_y(r.rdh, r.ysem.at[3])
    dhid = total(r.rdh)
    r.dhid[...] = dhid

    dtable = halves(mb(split(dhid * inv_degree, 0), r.counts[...]))
    back = jnp.concatenate([dtable[:, rows : rows + half], dtable[:, rows + half :]], 0).T
    r.out2[...] = back.reshape(r.out2.shape)
    rows_start(r.out2, r.mid2, r.rsem.at[3], r.zsem2)
    r.down[...] = dtable[:, :rows]

    dprob = mm(r.fresh[...], dhid)
    a_prob = r.aprob[...]
    dagent = a_prob * (dprob - jnp.sum(a_prob * dprob, 0, keepdims=True)) * scale
    dfresh_part = mt(dagent, xt) + mt(a_prob, dhid)
    r.give2[...] = jnp.concatenate(
        [dfresh_part, jnp.zeros((VN, LANES - HEAD), F32)], 1
    ).reshape(r.give2.shape)
    group_start(r.give2, r.got2, r.s2)
    r.dx[...] = dhid + mm(r.fresh_t[...], dagent)
    units = r.w_up.shape[1]
    grad_up = mt(hid_all, dpre)
    grad_down = mt(act, ct_all)

    def put3(row, value):
        r.give3[pl.ds(row, value.shape[0]), :] = value

    put3(0, grad_up)
    blocks = dim // LANES
    for b in range(blocks):
        put3(dim + b * units, grad_down[:, b * LANES : (b + 1) * LANES])
    base_value = dim + blocks * units
    base_latent = base_value + blocks * HEAD
    pad3 = r.give3.shape[0] - base_latent - VN
    if pad3:
        put3(base_latent + VN, jnp.zeros((pad3, LANES), F32))
    wait_x(r.got2, r.s2.at[1])
    r.piece2[...] = total(r.got2)
    z_share(r.piece2, r.gotz2, r.s2)
    rows_forward(0, r.mid2, r.land2, r.zsem2, r.rsem.at[4], r.rsem.at[5])
    wait_z(r.gotz2, r.s2.at[3])
    r.full2[xc] = total(r.gotz2)
    group_gather(r.full2, r.s2)
    wait_y(r.rbr, r.ysem.at[5])
    r.updated[...] = total(r.rbr).T
    if len(order) > 0:
        rows_forward(order[0], r.mid2, r.land2, r.zsem2, r.rsem.at[4], r.rsem.at[5])
    wait_x(r.full2, r.s2.at[5])
    dfresh = r.full2[...].reshape(VN, LANES)[:, :HEAD]

    prob = r.weights[...]
    vt = r.vt[:HEAD]
    dvt = mm(dfresh.T, prob)
    dweights = mm(dfresh, vt)
    centre = jnp.sum(dfresh * r.attended[...], 1, keepdims=True)
    dscores = prob * (dweights - centre) * scale
    dlatent = mt(dscores, xt)
    xt_flat = r.xt[...].reshape(dim, rows)
    grad_value = mt(dvt, xt_flat)
    for b in range(blocks):
        put3(base_value + b * HEAD, grad_value[:, b * LANES : (b + 1) * LANES])
    put3(base_latent, jnp.concatenate([dlatent, jnp.zeros((VN, LANES - HEAD), F32)], 1))
    rows3 = r.give3.shape[0] // nxc
    tile3 = rows3 // nz

    def piece3(i):
        return pl.ds(pl.multiple_of(i * rows3, 8), rows3)

    def start3(d):
        peer = x_peer(d)
        send(
            r.give3.at[piece3(peer)], r.got3.at[xc], r.s3.at[0], r.s3.at[1],
            {"graph": z * nxc + peer},
        )

    loop(1, nxc, start3)
    r.got3[xc] = r.give3[piece3(xc), :]
    r.dx[...] = r.dx[...] + mm(r.latents[...].T, dscores)
    dthrough_value = mm(r.w_value[...], dvt)
    for i in order[1:]:
        rows_forward(i, r.mid2, r.land2, r.zsem2, r.rsem.at[4], r.rsem.at[5])
    wait_x(r.got3, r.s3.at[1])
    r.piece3[...] = total(r.got3).reshape(nz, tile3, LANES)

    def scatter3(d):
        peer = z_peer(d)
        send(
            r.piece3.at[peer], r.gotz3.at[z], r.s3.at[2], r.s3.at[3],
            {"graph": peer * nxc + xc},
        )

    loop(1, nz, scatter3)
    r.gotz3[z] = r.piece3[z]
    wait_z(r.gotz3, r.s3.at[3])
    r.full3[xc, z] = total(r.gotz3)

    def gather3(d):
        send(
            r.full3.at[xc, z], r.full3.at[xc, z], r.s3.at[4], r.s3.at[5],
            {"graph": z_peer(d) * nxc + xc},
        )

    loop(1, nz, gather3)

    rows_wait(r.land2, r.rsem.at[5])
    far_back = packed_product(r.st[:, pl.ds(0, half)], r.st[:, pl.ds(half, half)], r.land2)
    dlocal = r.down[...] + halves(far_back)
    grad_local = mt(dlocal, xt_flat)
    r.give4[...] = jnp.concatenate(
        [grad_local[:, b * LANES : (b + 1) * LANES] for b in range(blocks)], 0
    ).reshape(r.give4.shape)
    group_start(r.give4, r.got4, r.s4)
    r.dtp[...] = (mm(r.w_local[...], dlocal) + dthrough_value).reshape(r.dtp.shape)
    y_send(lambda peer: r.dtp.at[peer], r.rdt, r.ysem.at[6], r.ysem.at[7])
    r.rdt[mp] = r.dtp[mp] + r.dx[...]
    wait(r.full3.at[0, pl.ds(0, nz - 1)], r.s3.at[5])

    def spread3(d):
        send(
            r.full3.at[xc], r.full3.at[xc], r.s3.at[6], r.s3.at[7],
            {"graph": z * nxc + x_peer(d)},
        )

    loop(1, nxc, spread3)
    wait_x(r.got4, r.s4.at[1])
    r.piece4[...] = total(r.got4)
    z_share(r.piece4, r.gotz4, r.s4)
    wait_y(r.rdt, r.ysem.at[7])
    r.grad_agents[...] = total(r.rdt).T
    wait_x(r.full3, r.s3.at[7])
    sums = r.full3[...].reshape(r.give3.shape) * factor
    r.grad_up[...] = sums[:dim]
    for b in range(blocks):
        r.grad_down[:, b * LANES : (b + 1) * LANES] = sums[dim + b * units : dim + (b + 1) * units]
    for b in range(blocks):
        low = base_value + b * HEAD
        r.grad_value[b * LANES : (b + 1) * LANES, :] = sums[low : low + HEAD].T
    r.grad_latents[...] = dfresh * factor + sums[base_latent : base_latent + VN, :HEAD]
    wait_z(r.gotz4, r.s4.at[3])
    r.full4[xc] = total(r.gotz4)
    group_gather(r.full4, r.s4)

    for give, got_z, sems in (
        (r.give1, r.gotz1, r.s1),
        (r.give2, r.gotz2, r.s2),
        (r.give4, r.gotz4, r.s4),
    ):
        wait_x(give, sems.at[0])
        wait_z(got_z, sems.at[2])
    wait_x(r.full1, r.s1.at[4])
    wait_x(r.full2, r.s2.at[4])
    wait_x(r.got3, r.s3.at[0])
    wait_z(r.gotz3, r.s3.at[2])
    wait(r.full3.at[0, pl.ds(0, nz - 1)], r.s3.at[4])
    wait_x(r.full3, r.s3.at[6])
    for mid, land, base in ((r.mid1, r.land1, 0), (r.mid2, r.land2, 3)):
        wait(mid.at[pl.ds(0, nz - 1)], r.rsem.at[base])
        wait(land.at[:, pl.ds(0, nxc - 1)], r.rsem.at[base + 1])
    for ref, i in ((r.hid, 0), (r.rdh, 2), (r.rbr, 4), (r.rdt, 6)):
        wait_y(ref, r.ysem.at[i])
    wait_x(r.full4, r.s4.at[5])
    final = r.full4[...].reshape(blocks * HEAD, LANES) * factor
    for b in range(blocks):
        r.grad_local[b * LANES : (b + 1) * LANES, :] = final[b * HEAD : (b + 1) * HEAD].T
    wait_x(r.full4, r.s4.at[4])


def on_device(
    nz, agents, latents, w_local, w_value, w_up, w_down, neighbours, degree, send_rows, cotangent
):
    rows, dim = agents.shape
    ng = lax.axis_size("graph")
    nmp = lax.axis_size("mp")
    nxc = ng // nz
    units = w_up.shape[1]
    sends = send_rows[0].reshape(ng, 2, 8).transpose(1, 0, 2).reshape(1, ng * SLOTS)
    inputs = dict(
        agents=agents,
        latents=latents,
        w_local=w_local,
        w_value=w_value,
        w_up=w_up,
        w_down=w_down,
        neighbours=neighbours,
        degree=degree.reshape(1, rows),
        sends=sends,
        cotangent=cotangent,
    )
    outs = dict(
        updated=(rows, HEAD),
        grad_agents=(rows, HEAD),
        grad_latents=(VN, HEAD),
        grad_local=(dim, HEAD),
        grad_value=(dim, HEAD),
        grad_up=(dim, units),
        grad_down=(units, dim),
    )
    half = ng * 8
    blocks = dim // LANES
    step = 8 * nz
    need = (dim + blocks * units + blocks * HEAD + VN) // nxc
    rows3 = -(-need // step) * step
    rows4 = blocks * HEAD // nxc
    rows1 = VN // nxc
    vmem = lambda *shape: pltpu.VMEM(shape, F32)
    dma = lambda n: pltpu.SemaphoreType.DMA((n,))
    scratch = dict(
        xt=vmem(nmp, HEAD, rows),
        lt2=pltpu.VMEM((2 * HEAD, rows), BF16),
        vt=vmem(2 * HEAD, rows),
        st=pltpu.VMEM((rows, 2 * half), BF16),
        counts=pltpu.VMEM((rows, rows + 2 * half), BF16),
        nbm=pltpu.VMEM((rows, SLOTS), jnp.int32),
        weights=vmem(VN, rows),
        aprob=vmem(VN, rows),
        attended=vmem(VN, HEAD),
        fresh=vmem(VN, HEAD),
        fresh_t=vmem(HEAD, VN),
        ct=vmem(nmp, HEAD, rows),
        dact=vmem(units, rows),
        wut=vmem(units, dim),
        wdt=vmem(dim, units),
        hid=vmem(nmp, HEAD, rows),
        dhp=vmem(nmp, HEAD, rows),
        rdh=vmem(nmp, HEAD, rows),
        brp=vmem(nmp, HEAD, rows),
        rbr=vmem(nmp, HEAD, rows),
        dtp=vmem(nmp, HEAD, rows),
        rdt=vmem(nmp, HEAD, rows),
        dhid=vmem(HEAD, rows),
        down=vmem(HEAD, rows),
        dx=vmem(HEAD, rows),
        give3=vmem(nxc * rows3, LANES),
        got3=vmem(nxc, rows3, LANES),
        piece3=vmem(nz, rows3 // nz, LANES),
        gotz3=vmem(nz, rows3 // nz, LANES),
        full3=vmem(nxc, nz, rows3 // nz, LANES),
        s3=dma(8),
        rsem=dma(6),
        zsem1=dma(4),
        zsem2=dma(4),
        ysem=dma(8),
    )
    for i in (1, 2):
        scratch["out%d" % i] = vmem(nz, nxc, 8, LANES)
        scratch["mid%d" % i] = vmem(nz, nxc, 8, LANES)
        scratch["land%d" % i] = vmem(nz, nxc, 8, LANES)
    for i, n in ((1, rows1), (2, rows1), (4, rows4)):
        scratch["give%d" % i] = vmem(nxc, n, LANES)
        scratch["got%d" % i] = vmem(nxc, n, LANES)
        scratch["piece%d" % i] = vmem(n, LANES)
        scratch["gotz%d" % i] = vmem(nz, n, LANES)
        scratch["full%d" % i] = vmem(nxc, n, LANES)
        scratch["s%d" % i] = dma(6)
    names = list(inputs) + list(outs) + list(scratch)
    spec = pl.BlockSpec(memory_space=pltpu.VMEM)
    result = pl.pallas_call(
        functools.partial(layer, nz, nxc, nmp, rows, dim, names),
        out_shape=[jax.ShapeDtypeStruct(shape, F32) for shape in outs.values()],
        in_specs=[spec] * len(inputs),
        out_specs=[spec] * len(outs),
        scratch_shapes=list(scratch.values()),
        compiler_params=pltpu.CompilerParams(
            collective_id=0, has_side_effects=True, vmem_limit_bytes=40 * 1024 * 1024
        ),
        name="layer",
    )(*inputs.values())
    return tuple(result)


def solution(mesh, nz=16):
    return jax.shard_map(
        functools.partial(on_device, nz),
        mesh=mesh,
        in_specs=(
            P("graph", None),
            P(None, "mp"),
            P(None, "mp"),
            P(None, "mp"),
            P(None, "mp"),
            P("mp", None),
            P("graph", None),
            P("graph"),
            P("graph", None, None),
            P("graph", None),
        ),
        out_specs=(
            P("graph", "mp"),
            P("graph", "mp"),
            P(None, "mp"),
            P(None, "mp"),
            P(None, "mp"),
            P(None, "mp"),
            P("mp", None),
        ),
        check_vma=False,
    )
```

```python
import functools
import math
from types import SimpleNamespace

import jax
import jax.numpy as jnp
from jax import lax
from jax.experimental import pallas as pl
from jax.experimental.pallas import tpu as pltpu
from jax.sharding import PartitionSpec as P

HEAD = 64
VN = 64
SLOTS = 16
LANES = 128
MESH = pl.DeviceIdType.MESH
F32 = jnp.float32
BF16 = jnp.bfloat16


def dot(left, right, contract, precision):
    return lax.dot_general(
        left, right, (contract, ((), ())), precision=precision, preferred_element_type=F32
    )


def mm(left, right):
    return dot(left, right, ((1,), (0,)), lax.Precision.HIGHEST)


def mt(left, right):
    return dot(left, right, ((1,), (1,)), lax.Precision.HIGHEST)


def mb(left, right):
    return dot(left, right, ((1,), (0,)), lax.Precision.DEFAULT)


def mbt(left, right):
    return dot(left, right, ((1,), (1,)), lax.Precision.DEFAULT)


def split(x, axis):
    high = x.astype(BF16)
    low = (x - high.astype(F32)).astype(BF16)
    return jnp.concatenate([high, low], axis)


def halves(x):
    half = x.shape[0] // 2
    return x[:half] + x[half:]


def layer(nz, nxc, nmp, rows, dim, names, given, *refs):
    r = SimpleNamespace(**dict(zip(names, refs)))
    loads = {
        name: pltpu.make_async_copy(getattr(r, name + "_hbm"), getattr(r, name), r.lsem.at[i])
        for i, name in enumerate(given)
    }
    for load in loads.values():
        load.start()
    graph = lax.axis_index("graph")
    mp = lax.axis_index("mp")
    z = graph // nxc
    xc = lax.rem(graph, nxc)
    nb4 = nz // 4
    zb = z // 4
    zm = lax.rem(z, 4)
    ng = nz * nxc
    scale = 1.0 / math.sqrt(HEAD)
    factor = 1.0 / math.sqrt(rows * ng)

    def z_peer(d):
        return lax.rem(z + d, nz)

    def x_peer(d):
        return lax.rem(xc + d, nxc)

    def send(src, dst, ssem, rsem, device):
        pltpu.make_async_remote_copy(
            src_ref=src,
            dst_ref=dst,
            send_sem=ssem,
            recv_sem=rsem,
            device_id=device,
            device_id_type=MESH,
        ).start()

    def wait(ref, sem):
        pltpu.make_async_copy(ref, ref, sem).wait()

    def loop(low, high, body):
        def step(d, carry):
            body(d)
            return carry

        lax.fori_loop(low, high, step, 0)

    barrier = pltpu.get_barrier_semaphore()

    def greet(device):
        pl.semaphore_signal(barrier, inc=1, device_id=device, device_id_type=MESH)

    loop(1, nz, lambda d: greet({"graph": z_peer(d) * nxc + xc}))
    loop(1, nxc, lambda d: greet({"graph": z * nxc + x_peer(d)}))
    loop(1, nmp, lambda d: greet({"mp": lax.rem(mp + d, nmp)}))

    def group_start(give, got, sems):
        def go(d):
            peer = x_peer(d)
            send(give.at[peer], got.at[xc], sems.at[0], sems.at[1], {"graph": z * nxc + peer})

        loop(1, nxc, go)
        got[xc] = give[xc]

    def z_share(piece, got, sems):
        def go(d):
            send(piece, got.at[z], sems.at[2], sems.at[3], {"graph": z_peer(d) * nxc + xc})

        loop(1, nz, go)
        got[z] = piece[...]

    def group_gather(full, sems):
        def go(d):
            send(full.at[xc], full.at[xc], sems.at[4], sems.at[5], {"graph": z * nxc + x_peer(d)})

        loop(1, nxc, go)

    def wait_x(ref, sem):
        wait(ref.at[pl.ds(0, nxc - 1)], sem)

    def wait_z(ref, sem):
        wait(ref.at[pl.ds(0, nz - 1)], sem)

    def total(ref):
        acc = ref[0]
        for i in range(1, ref.shape[0]):
            acc = acc + ref[i]
        return acc

    def merged(ref):
        count = ref.shape[0]
        parts = [ref[i] for i in range(count)]
        tops = [part[:, 96:97] for part in parts]
        top = functools.reduce(jnp.maximum, tops)
        acc = parts[0] * jnp.exp(tops[0] - top)
        for i in range(1, count):
            acc = acc + parts[i] * jnp.exp(tops[i] - top)
        lane = lax.broadcasted_iota(jnp.int32, acc.shape, 1)
        return jnp.where(lane >= 96, top, acc)

    def rows_x(i, out, mid, xs, xr):
        base = lax.rem(zb + nb4 - i, nb4) * 4

        def go(d):
            peer = x_peer(d)
            send(
                out.at[pl.ds(base, 4), peer],
                mid.at[pl.ds(base, 4), xc],
                xs,
                xr.at[i],
                {"graph": z * nxc + peer},
            )

        loop(1, nxc, go)
        mid[pl.ds(base, 4), xc] = out[pl.ds(base, 4), xc]

    def rows_z(i, mid, land, xr, zs, zr):
        base = lax.rem(zb + nb4 - i, nb4) * 4
        wait(mid.at[pl.ds(0, 4), pl.ds(0, nxc - 1)], xr.at[i])
        for d in range(1 if i == 0 else 0, 4):
            peer = base + lax.rem(zm + d, 4)
            send(mid.at[peer], land.at[z], zs, zr, {"graph": peer * nxc + xc})
        if i == 0:
            land[z] = mid[z]

    def rows_wait(land, zr):
        wait(land.at[pl.ds(0, nz - 1)], zr)

    def y_send(src_of, got, ssem, rsem):
        for d in range(1, nmp):
            peer = lax.rem(mp + d, nmp)
            send(src_of(peer), got.at[mp], ssem, rsem, {"mp": peer})

    def wait_y(ref, sem):
        wait(ref.at[pl.ds(0, nmp - 1)], sem)

    order = {1: (0,), 2: (1, 0), 4: (2, 1, 3, 0)}[nb4]
    rows1 = (r.mid1, r.land1, r.xsem1, r.rsem.at[1], r.rsem.at[2])
    rows2 = (r.mid2, r.land2, r.xsem2, r.rsem.at[4], r.rsem.at[5])

    half = ng * 8
    loads["agents"].wait()
    xt_all = r.agents[...].T
    r.xt[...] = xt_all.reshape(nmp, HEAD, rows)
    xt = r.xt[mp]
    xt2 = split(xt, 0)
    r.xt2[...] = xt2
    spread = lax.broadcasted_iota(jnp.int32, (ng, half), 1) // 8 == lax.broadcasted_iota(
        jnp.int32, (ng, half), 0
    )
    spread = jnp.where(spread, 1.0, 0.0).astype(BF16)
    loads["sends"].wait()
    wide = mb(r.sends[...].astype(F32).astype(BF16), spread)
    own_slot = lax.broadcasted_iota(jnp.int32, (8, half), 1) % 8 == lax.broadcasted_iota(
        jnp.int32, (8, half), 0
    )
    chunk = 256
    for h in range(2):
        line = jnp.sum(jnp.where(own_slot, wide[h * 8 : h * 8 + 8], 0.0), 0, keepdims=True)
        line = line.astype(jnp.int32)
        for c in range(half // chunk):
            row_id = lax.broadcasted_iota(jnp.int32, (rows, chunk), 0)
            hit = row_id == line[:, c * chunk : (c + 1) * chunk]
            r.st[:, pl.ds(h * half + c * chunk, chunk)] = jnp.where(hit, 1.0, 0.0).astype(BF16)
    rows_out = halves(mb(xt2, r.st[...]))
    packed = jnp.concatenate([rows_out[:, :half], rows_out[:, half:]], 0).T
    r.out1[...] = packed.reshape(nz, nxc, 8, LANES)

    loads["w_value_t"].wait()
    r.vt[:HEAD] = mm(r.w_value_t[...], xt_all)
    r.vt[HEAD:] = jnp.ones((HEAD, rows), F32)
    loads["latents"].wait()
    scores = mm(r.latents[...], xt) * scale
    local_top = jnp.max(scores, 1, keepdims=True)
    weights = jnp.exp(scores - local_top)
    r.weights[...] = weights
    part = mt(weights, r.vt[...])
    lane = lax.broadcasted_iota(jnp.int32, part.shape, 1)
    r.give1[...] = jnp.where(lane >= 96, local_top, part).reshape(r.give1.shape)
    pl.semaphore_wait(barrier, nz + nxc + nmp - 3)
    group_start(r.give1, r.got1, r.s1)
    for i in order:
        rows_x(i, r.out1, r.mid1, r.rsem.at[0], r.xsem1)

    loads["degree"].wait()
    loads["neighbours_t"].wait()
    degree = r.degree[...].astype(F32)
    inv_degree = 1.0 / degree
    slot = lax.broadcasted_iota(jnp.int32, (SLOTS, rows), 0)
    near = r.neighbours_t[...]
    far = near - rows
    k = far & 15
    far_col = rows + (k >> 3) * half + (far >> 4) * 8 + (k & 7)
    column = jnp.where(near < rows, near, far_col)
    column = jnp.where(slot < r.degree[...], column, -1)
    r.nbm[...] = column.astype(F32).T.astype(jnp.int32)
    width = rows + 2 * half
    part_width = 768 if width % 768 == 0 else 256

    def count_rows(b):
        row = pl.multiple_of(b * 16, 16)
        nb = r.nbm[pl.ds(row, 16), :]
        for c in range(width // part_width):
            col = lax.broadcasted_iota(jnp.int32, (16, part_width), 1) + c * part_width
            acc = jnp.zeros((16, part_width), F32)
            for s in range(SLOTS):
                acc = acc + jnp.where(nb[:, s : s + 1] == col, 1.0, 0.0)
            r.counts[pl.ds(row, 16), pl.ds(c * part_width, part_width)] = acc.astype(BF16)

    def count_part(p):
        blocks = rows // 64
        loop(p * blocks, (p + 1) * blocks, count_rows)

    wait_x(r.got1, r.s1.at[1])
    r.piece1[...] = merged(r.got1)
    z_share(r.piece1, r.gotz1, r.s1)
    for i in order:
        rows_z(i, *rows1)
    count_part(0)
    loads["w_local_t"].wait()
    r.wlt[mp] = r.w_local_t[...]
    y_send(lambda peer: r.w_local_t, r.wlt, r.ysem.at[0], r.ysem.at[1])
    count_part(1)
    count_part(2)
    loads["cotangent"].wait()
    loads["w_down"].wait()
    loads["w_up"].wait()
    ct_all = r.cotangent[...].T
    r.ct[...] = ct_all.reshape(nmp, HEAD, rows)
    r.dact[...] = mm(r.w_down[...], ct_all)
    r.wut[...] = r.w_up[...].T
    r.wdt[...] = r.w_down[...].T
    wait_z(r.gotz1, r.s1.at[3])
    r.full1[xc] = merged(r.gotz1)
    group_gather(r.full1, r.s1)
    count_part(3)
    wait_y(r.wlt, r.ysem.at[1])
    wl_t = r.wlt[...].reshape(dim, dim)
    wl = wl_t.T
    r.wl[...] = wl.reshape(nmp, HEAD, dim)
    r.wlu[...] = mm(wl, r.w_up[...])
    r.dmean_ct[...] = mm(r.wl[mp], ct_all)
    own = mbt(xt2, r.counts[:, pl.ds(0, rows)])

    wait_x(r.full1, r.s1.at[5])
    soft = r.full1[...].reshape(VN, LANES)
    inv_total = 1.0 / soft[:, 64:65]
    attended = soft[:, :HEAD] * inv_total
    prob = weights * (jnp.exp(local_top - soft[:, 96:97]) * inv_total)
    r.prob[...] = prob
    r.attended[...] = attended
    fresh = r.latents[...] + attended
    r.fresh[...] = fresh
    a_scores = mm(fresh, xt) * scale
    a_exp = jnp.exp(a_scores - jnp.max(a_scores, 0, keepdims=True))
    a_prob = a_exp / jnp.sum(a_exp, 0, keepdims=True)
    r.aprob[...] = a_prob
    r.fresh_t[...] = fresh.T
    r.read[mp] = mm(r.fresh_t[...], a_prob)
    y_send(lambda peer: r.read.at[mp], r.read, r.ysem.at[2], r.ysem.at[3])

    def put3(row, value):
        r.give3[pl.ds(row, value.shape[0]), :] = value

    blocks = dim // LANES
    units = r.w_up.shape[1]
    base_local = dim + blocks * units
    base_prob = base_local + blocks * HEAD
    end3 = base_prob + blocks * VN
    weighted_x = mt(prob, xt_all)
    for b in range(blocks):
        put3(base_prob + b * VN, weighted_x[:, b * LANES : (b + 1) * LANES])
    if r.give3.shape[0] > end3:
        put3(end3, jnp.zeros((r.give3.shape[0] - end3, LANES), F32))
    wait_y(r.read, r.ysem.at[3])
    partial_hidden = xt_all + r.read[...].reshape(dim, rows)

    def packed_product(left_low, left_high, land):
        both = split(land[...].reshape(half, LANES), 1)
        low = mb(left_low, both)
        high = mb(left_high, both)
        lane2 = lax.broadcasted_iota(jnp.int32, low.shape, 1) % LANES
        picked = jnp.where(lane2 < HEAD, low, high)
        return (picked[:, :LANES] + picked[:, LANES:]).T

    rows_wait(r.land1, r.rsem.at[2])
    far_sum = packed_product(
        r.counts[:, pl.ds(rows, half)], r.counts[:, pl.ds(rows + half, half)], r.land1
    )
    r.mean[mp] = halves(own + far_sum) * inv_degree
    y_send(lambda peer: r.mean.at[mp], r.mean, r.ysem.at[4], r.ysem.at[5])
    wait_y(r.mean, r.ysem.at[5])

    mean_all = r.mean[...].reshape(dim, rows)
    hid_all = partial_hidden + mm(wl_t, mean_all)
    pre = mm(r.wut[...], hid_all)
    gate = 1.0 / (1.0 + jnp.exp(-pre))
    dpre = r.dact[...] * (gate * (1.0 + pre * (1.0 - gate)))
    r.dmp[...] = mm(r.wlu[...], dpre).reshape(r.dmp.shape)
    y_send(lambda peer: r.dmp.at[peer], r.rdm, r.ysem.at[6], r.ysem.at[7])
    r.dhp[...] = mm(r.w_up[...], dpre).reshape(r.dhp.shape)
    y_send(lambda peer: r.dhp.at[peer], r.rdh, r.ysem.at[8], r.ysem.at[9])
    act = pre * gate
    r.brp[...] = mm(r.wdt[...], act).reshape(r.brp.shape)
    y_send(lambda peer: r.brp.at[peer], r.rbr, r.ysem.at[10], r.ysem.at[11])
    r.rdm[mp] = r.dmp[mp] + r.dmean_ct[...]
    r.rdh[mp] = r.dhp[mp] + r.ct[mp]
    r.hid[...] = hid_all.reshape(r.hid.shape)
    r.rbr[mp] = r.brp[mp] + r.hid[mp]
    put3(0, mt(hid_all, dpre))
    grad_down = mt(act, ct_all)
    for b in range(blocks):
        put3(dim + b * units, grad_down[:, b * LANES : (b + 1) * LANES])
    wait_y(r.rdm, r.ysem.at[7])
    dmean = total(r.rdm) * inv_degree

    dtable = halves(mb(split(dmean, 0), r.counts[...]))
    back = jnp.concatenate([dtable[:, rows : rows + half], dtable[:, rows + half :]], 0).T
    r.out2[...] = back.reshape(r.out2.shape)
    for i in order:
        rows_x(i, r.out2, r.mid2, r.rsem.at[3], r.xsem2)
    wait_y(r.rdh, r.ysem.at[9])
    dhid = total(r.rdh)
    r.dx[...] = dhid + dtable[:, :rows]

    dprob = mm(r.fresh[...], dhid)
    a_prob = r.aprob[...]
    dagent = a_prob * (dprob - jnp.sum(a_prob * dprob, 0, keepdims=True)) * scale
    dfresh_part = mt(dagent, xt) + mt(a_prob, dhid)
    no_lanes = jnp.zeros((VN, LANES - HEAD), F32)
    r.give2[...] = jnp.concatenate([dfresh_part, no_lanes], 1).reshape(r.give2.shape)
    group_start(r.give2, r.got2, r.s2)
    wait_x(r.got2, r.s2.at[1])
    r.piece2[...] = total(r.got2)
    z_share(r.piece2, r.gotz2, r.s2)
    for i in order:
        rows_z(i, *rows2)
    grad_local = mt(dhid, mean_all)
    for b in range(blocks):
        put3(base_local + b * HEAD, grad_local[:, b * LANES : (b + 1) * LANES])
    rows3 = r.give3.shape[0] // nxc
    tile3 = rows3 // nz

    def piece3(i):
        return pl.ds(pl.multiple_of(i * rows3, 8), rows3)

    def start3(d):
        peer = x_peer(d)
        send(
            r.give3.at[piece3(peer)], r.got3.at[xc], r.s3.at[0], r.s3.at[1],
            {"graph": z * nxc + peer},
        )

    loop(1, nxc, start3)
    r.got3[xc] = r.give3[piece3(xc), :]
    r.dx[...] = r.dx[...] + mm(r.fresh_t[...], dagent)
    wait_x(r.got3, r.s3.at[1])
    r.piece3[...] = total(r.got3).reshape(nz, tile3, LANES)

    def scatter3(d):
        peer = z_peer(d)
        send(
            r.piece3.at[peer], r.gotz3.at[z], r.s3.at[2], r.s3.at[3],
            {"graph": peer * nxc + xc},
        )

    loop(1, nz, scatter3)
    r.gotz3[z] = r.piece3[z]
    wait_z(r.gotz2, r.s2.at[3])
    r.full2[xc] = total(r.gotz2)
    group_gather(r.full2, r.s2)
    wait_y(r.rbr, r.ysem.at[11])
    r.updated_t[...] = total(r.rbr)
    wait_x(r.full2, r.s2.at[5])
    dfresh = r.full2[...].reshape(VN, LANES)[:, :HEAD]

    dweights = mm(dfresh, r.vt[:HEAD])
    centre = jnp.sum(dfresh * r.attended[...], 1, keepdims=True)
    prob = r.prob[...]
    dscores = prob * (dweights - centre) * scale
    dlatent = mt(dscores, xt)
    r.give4[...] = jnp.concatenate([dlatent, no_lanes], 1).reshape(r.give4.shape)
    group_start(r.give4, r.got4, r.s4)
    dfresh_t = dfresh.T
    dvt = mm(dfresh_t, prob)
    r.dtp[...] = dot(
        r.w_value_t[...], dvt, ((0,), (0,)), lax.Precision.HIGHEST
    ).reshape(r.dtp.shape)
    y_send(lambda peer: r.dtp.at[peer], r.rdt, r.ysem.at[12], r.ysem.at[13])
    r.rdt[mp] = r.dtp[mp] + r.dx[...] + mm(r.latents[...].T, dscores)
    wait_x(r.got4, r.s4.at[1])
    r.piece4[...] = total(r.got4)
    z_share(r.piece4, r.gotz4, r.s4)
    wait_z(r.gotz3, r.s3.at[3])
    r.full3[xc, z] = total(r.gotz3)

    def gather3(d):
        send(
            r.full3.at[xc, z], r.full3.at[xc, z], r.s3.at[4], r.s3.at[5],
            {"graph": z_peer(d) * nxc + xc},
        )

    loop(1, nz, gather3)
    wait_z(r.gotz4, r.s4.at[3])
    r.full4[xc] = total(r.gotz4)
    group_gather(r.full4, r.s4)
    wait(r.full3.at[0, pl.ds(0, nz - 1)], r.s3.at[5])

    def spread3(d):
        send(
            r.full3.at[xc], r.full3.at[xc], r.s3.at[6], r.s3.at[7],
            {"graph": z * nxc + x_peer(d)},
        )

    loop(1, nxc, spread3)
    wait_y(r.rdt, r.ysem.at[13])
    dx = total(r.rdt)

    rows_wait(r.land2, r.rsem.at[5])
    far_back = packed_product(r.st[:, pl.ds(0, half)], r.st[:, pl.ds(half, half)], r.land2)
    r.grad_agents_t[...] = dx + halves(far_back)
    wait_x(r.full4, r.s4.at[5])
    r.grad_latents[...] = (dfresh + r.full4[...].reshape(VN, LANES)[:, :HEAD]) * factor
    wait_x(r.full3, r.s3.at[7])
    sums = r.full3[...].reshape(r.give3.shape)
    r.grad_up[...] = sums[:dim] * factor
    for b in range(blocks):
        cols = pl.ds(b * LANES, LANES)
        r.grad_down[:, cols] = sums[dim + b * units : dim + (b + 1) * units] * factor
        low = base_local + b * HEAD
        r.grad_local_t[:, cols] = sums[low : low + HEAD] * factor
        low = base_prob + b * VN
        r.grad_value_t[:, cols] = mm(dfresh_t, sums[low : low + VN]) * factor

    for give, got_z, full, sems in (
        (r.give1, r.gotz1, r.full1, r.s1),
        (r.give2, r.gotz2, r.full2, r.s2),
        (r.give4, r.gotz4, r.full4, r.s4),
    ):
        wait_x(give, sems.at[0])
        wait_z(got_z, sems.at[2])
        wait_x(full, sems.at[4])
    wait_x(r.got3, r.s3.at[0])
    wait_z(r.gotz3, r.s3.at[2])
    wait(r.full3.at[0, pl.ds(0, nz - 1)], r.s3.at[4])
    wait_x(r.full3, r.s3.at[6])
    for mid, land, base in ((r.mid1, r.land1, 0), (r.mid2, r.land2, 3)):
        wait(mid.at[:, pl.ds(0, nxc - 1)], r.rsem.at[base])
        wait(land.at[pl.ds(0, nz - 1)], r.rsem.at[base + 1])
    wait_y(r.wlt, r.ysem.at[0])
    for i, ref in enumerate((r.read, r.mean, r.rdm, r.rdh, r.rbr, r.rdt)):
        wait_y(ref, r.ysem.at[2 + 2 * i])


def store(*refs):
    count = len(refs) // 2
    sems = refs[-1]
    copies = [
        pltpu.make_async_copy(refs[i], refs[count + i], sems.at[i]) for i in range(count)
    ]
    for copy in copies:
        copy.start()
    for copy in copies:
        copy.wait()


def on_device(
    nz, agents, latents, w_local, w_value, w_up, w_down, neighbours, degree, send_rows, cotangent
):
    rows, dim = agents.shape
    ng = lax.axis_size("graph")
    nmp = lax.axis_size("mp")
    nxc = ng // nz
    units = w_up.shape[1]
    inputs = dict(
        agents=agents,
        latents=latents,
        w_local_t=w_local.T,
        w_value_t=w_value.T,
        w_up=w_up,
        w_down=w_down,
        neighbours_t=neighbours.T,
        degree=degree.reshape(1, rows),
        sends=send_rows[0].T,
        cotangent=cotangent,
    )
    outs = dict(
        updated_t=(HEAD, rows),
        grad_agents_t=(HEAD, rows),
        grad_latents=(VN, HEAD),
        grad_local_t=(HEAD, dim),
        grad_value_t=(HEAD, dim),
        grad_up=(dim, units),
        grad_down=(units, dim),
    )
    half = ng * 8
    blocks = dim // LANES
    step = 8 * nz
    need = (dim + blocks * (units + HEAD + VN)) // nxc
    rows3 = -(-need // step) * step
    rows1 = VN // nxc
    vmem = lambda *shape: pltpu.VMEM(shape, F32)
    dma = lambda n: pltpu.SemaphoreType.DMA((n,))
    scratch = dict(
        xt2=pltpu.VMEM((2 * HEAD, rows), BF16),
        vt=vmem(2 * HEAD, rows),
        st=pltpu.VMEM((rows, 2 * half), BF16),
        counts=pltpu.VMEM((rows, rows + 2 * half), BF16),
        nbm=pltpu.VMEM((rows, SLOTS), jnp.int32),
        weights=vmem(VN, rows),
        prob=vmem(VN, rows),
        aprob=vmem(VN, rows),
        attended=vmem(VN, HEAD),
        fresh=vmem(VN, HEAD),
        fresh_t=vmem(HEAD, VN),
        dact=vmem(units, rows),
        wut=vmem(units, dim),
        wdt=vmem(dim, units),
        wlt=vmem(nmp, HEAD, dim),
        wl=vmem(nmp, HEAD, dim),
        wlu=vmem(dim, units),
        dmean_ct=vmem(HEAD, rows),
        dx=vmem(HEAD, rows),
        xt=vmem(nmp, HEAD, rows),
        ct=vmem(nmp, HEAD, rows),
        read=vmem(nmp, HEAD, rows),
        mean=vmem(nmp, HEAD, rows),
        hid=vmem(nmp, HEAD, rows),
        dmp=vmem(nmp, HEAD, rows),
        rdm=vmem(nmp, HEAD, rows),
        dhp=vmem(nmp, HEAD, rows),
        rdh=vmem(nmp, HEAD, rows),
        brp=vmem(nmp, HEAD, rows),
        rbr=vmem(nmp, HEAD, rows),
        dtp=vmem(nmp, HEAD, rows),
        rdt=vmem(nmp, HEAD, rows),
        give3=vmem(nxc * rows3, LANES),
        got3=vmem(nxc, rows3, LANES),
        piece3=vmem(nz, rows3 // nz, LANES),
        gotz3=vmem(nz, rows3 // nz, LANES),
        full3=vmem(nxc, nz, rows3 // nz, LANES),
        s3=dma(8),
        rsem=dma(6),
        xsem1=dma(4),
        xsem2=dma(4),
        ysem=dma(14),
    )
    for i in (1, 2):
        scratch["out%d" % i] = vmem(nz, nxc, 8, LANES)
        scratch["mid%d" % i] = vmem(nz, nxc, 8, LANES)
        scratch["land%d" % i] = vmem(nz, nxc, 8, LANES)
    for i, n in ((1, rows1), (2, rows1), (4, rows1)):
        scratch["give%d" % i] = vmem(nxc, n, LANES)
        scratch["got%d" % i] = vmem(nxc, n, LANES)
        scratch["piece%d" % i] = vmem(n, LANES)
        scratch["gotz%d" % i] = vmem(nz, n, LANES)
        scratch["full%d" % i] = vmem(nxc, n, LANES)
        scratch["s%d" % i] = dma(6)
    for name, value in inputs.items():
        scratch[name] = pltpu.VMEM(value.shape, value.dtype)
    scratch["lsem"] = dma(len(inputs))
    names = [name + "_hbm" for name in inputs] + list(outs) + list(scratch)
    spec = pl.BlockSpec(memory_space=pltpu.VMEM)
    far_spec = pl.BlockSpec(memory_space=pltpu.HBM)
    result = pl.pallas_call(
        functools.partial(layer, nz, nxc, nmp, rows, dim, names, list(inputs)),
        out_shape=[jax.ShapeDtypeStruct(shape, F32) for shape in outs.values()],
        in_specs=[far_spec] * len(inputs),
        out_specs=[spec] * len(outs),
        scratch_shapes=list(scratch.values()),
        compiler_params=pltpu.CompilerParams(
            collective_id=0, has_side_effects=True, vmem_limit_bytes=62_000_000
        ),
        name="layer",
    )(*inputs.values())
    result = pl.pallas_call(
        store,
        out_shape=[jax.ShapeDtypeStruct(shape, F32) for shape in outs.values()],
        in_specs=[spec] * len(outs),
        out_specs=[far_spec] * len(outs),
        scratch_shapes=[dma(len(outs))],
        compiler_params=pltpu.CompilerParams(vmem_limit_bytes=62_000_000),
        name="store",
    )(*result)
    updated, grad_agents, grad_latents, grad_local, grad_value, grad_up, grad_down = result
    return (
        updated.T,
        grad_agents.T,
        grad_latents,
        grad_local.T,
        grad_value.T,
        grad_up,
        grad_down,
    )


def solution(mesh, nz=16):
    return jax.shard_map(
        functools.partial(on_device, nz),
        mesh=mesh,
        in_specs=(
            P("graph", None),
            P(None, "mp"),
            P(None, "mp"),
            P(None, "mp"),
            P(None, "mp"),
            P("mp", None),
            P("graph", None),
            P("graph"),
            P("graph", None, None),
            P("graph", None),
        ),
        out_specs=(
            P("graph", "mp"),
            P("graph", "mp"),
            P(None, "mp"),
            P(None, "mp"),
            P(None, "mp"),
            P(None, "mp"),
            P("mp", None),
        ),
        check_vma=False,
    )
```

```python
import functools
import math
from types import SimpleNamespace

import jax
import jax.numpy as jnp
from jax import lax
from jax.experimental import pallas as pl
from jax.experimental.pallas import tpu as pltpu
from jax.sharding import PartitionSpec as P

HEAD = 64
VN = 64
SLOTS = 16
LANES = 128
MESH = pl.DeviceIdType.MESH
F32 = jnp.float32
BF16 = jnp.bfloat16


def dot(left, right, contract, precision):
    return lax.dot_general(
        left, right, (contract, ((), ())), precision=precision, preferred_element_type=F32
    )


def mm(left, right):
    return dot(left, right, ((1,), (0,)), lax.Precision.HIGHEST)


def mt(left, right):
    return dot(left, right, ((1,), (1,)), lax.Precision.HIGHEST)


def mb(left, right):
    return dot(left, right, ((1,), (0,)), lax.Precision.DEFAULT)


def mbt(left, right):
    return dot(left, right, ((1,), (1,)), lax.Precision.DEFAULT)


def split(x, axis):
    high = x.astype(BF16)
    low = (x - high.astype(F32)).astype(BF16)
    return jnp.concatenate([high, low], axis)


def halves(x):
    half = x.shape[0] // 2
    return x[:half] + x[half:]


def layer(nz, nxc, nmp, rows, dim, names, given, *refs):
    r = SimpleNamespace(**dict(zip(names, refs)))
    loads = {
        name: pltpu.make_async_copy(getattr(r, name + "_hbm"), getattr(r, name), r.lsem.at[i])
        for i, name in enumerate(given)
    }
    for load in loads.values():
        load.start()
    graph = lax.axis_index("graph")
    mp = lax.axis_index("mp")
    z = graph // nxc
    xc = lax.rem(graph, nxc)
    nb4 = nz // 4
    zb = z // 4
    zm = lax.rem(z, 4)
    ng = nz * nxc
    scale = 1.0 / math.sqrt(HEAD)
    factor = 1.0 / math.sqrt(rows * ng)

    def z_peer(d):
        return lax.rem(z + d, nz)

    def x_peer(d):
        return lax.rem(xc + d, nxc)

    def send(src, dst, ssem, rsem, device):
        pltpu.make_async_remote_copy(
            src_ref=src,
            dst_ref=dst,
            send_sem=ssem,
            recv_sem=rsem,
            device_id=device,
            device_id_type=MESH,
        ).start()

    def wait(ref, sem):
        pltpu.make_async_copy(ref, ref, sem).wait()

    def loop(low, high, body):
        def step(d, carry):
            body(d)
            return carry

        lax.fori_loop(low, high, step, 0)

    barrier = pltpu.get_barrier_semaphore()

    def greet(device):
        pl.semaphore_signal(barrier, inc=1, device_id=device, device_id_type=MESH)

    loop(1, nz, lambda d: greet({"graph": z_peer(d) * nxc + xc}))
    loop(1, nxc, lambda d: greet({"graph": z * nxc + x_peer(d)}))
    loop(1, nmp, lambda d: greet({"mp": lax.rem(mp + d, nmp)}))

    def group_start(give, got, sems):
        def go(d):
            peer = x_peer(d)
            send(give.at[peer], got.at[xc], sems.at[0], sems.at[1], {"graph": z * nxc + peer})

        loop(1, nxc, go)
        got[xc] = give[xc]

    def z_share(piece, got, sems):
        def go(d):
            send(piece, got.at[z], sems.at[2], sems.at[3], {"graph": z_peer(d) * nxc + xc})

        loop(1, nz, go)
        got[z] = piece[...]

    def group_gather(full, sems):
        def go(d):
            send(full.at[xc], full.at[xc], sems.at[4], sems.at[5], {"graph": z * nxc + x_peer(d)})

        loop(1, nxc, go)

    def wait_x(ref, sem):
        wait(ref.at[pl.ds(0, nxc - 1)], sem)

    def wait_z(ref, sem):
        wait(ref.at[pl.ds(0, nz - 1)], sem)

    def put_packed(ref, value):
        packed = jnp.concatenate([value[: VN // 2], value[VN // 2 :]], 1)
        n = ref.shape[1]
        for i in range(ref.shape[0]):
            ref[i] = packed[i * n : (i + 1) * n]

    def get_packed(ref):
        packed = jnp.concatenate([ref[i] for i in range(ref.shape[0])], 0)
        return jnp.concatenate([packed[:, :HEAD], packed[:, HEAD:]], 0)

    def total(ref):
        acc = ref[0]
        for i in range(1, ref.shape[0]):
            acc = acc + ref[i]
        return acc

    def merged(ref):
        count = ref.shape[0]
        parts = [ref[i] for i in range(count)]
        tops = [part[:, 96:97] for part in parts]
        top = functools.reduce(jnp.maximum, tops)
        acc = parts[0] * jnp.exp(tops[0] - top)
        for i in range(1, count):
            acc = acc + parts[i] * jnp.exp(tops[i] - top)
        lane = lax.broadcasted_iota(jnp.int32, acc.shape, 1)
        return jnp.where(lane >= 96, top, acc)

    def rows_x(i, out, mid, xs, xr):
        base = lax.rem(zb + nb4 - i, nb4) * 4

        def go(d):
            peer = x_peer(d)
            send(
                out.at[pl.ds(base, 4), peer],
                mid.at[pl.ds(base, 4), xc],
                xs,
                xr.at[i],
                {"graph": z * nxc + peer},
            )

        loop(1, nxc, go)
        mid[pl.ds(base, 4), xc] = out[pl.ds(base, 4), xc]

    def rows_z(i, mid, land, via, xr, zs, zr, rs):
        base = lax.rem(zb + nb4 - i, nb4) * 4
        wait(mid.at[pl.ds(0, 4), pl.ds(0, nxc - 1)], xr.at[i])
        for d in range(1 if i == 0 else 0, 4):
            peer = base + lax.rem(zm + d, 4)
            device = {"graph": peer * nxc + xc}
            if i == nb4 // 2 and d == 0:
                send(mid.at[peer, upper], via, rs.at[0], rs.at[1], {"graph": z_peer(nz - 1) * nxc + xc})
                send(mid.at[peer, lower], land.at[z, lower], zs, zr, device)
            else:
                send(mid.at[peer], land.at[z], zs, zr, device)
        if i == 0:
            land[z] = mid[z]

    lower = pl.ds(0, nxc // 2)
    upper = pl.ds(nxc // 2, nxc - nxc // 2)

    def rows_relay(mid, land, via, xr, zs, zr, rs):
        wait(via, rs.at[1])
        send(
            via, land.at[z_peer(1), upper], zs, zr,
            {"graph": z_peer(nz // 2 + 1) * nxc + xc},
        )

    def rows_wait(land, zr):
        wait(land.at[pl.ds(0, nz - 1)], zr)

    def y_send(src_of, got, ssem, rsem):
        for d in range(1, nmp):
            peer = lax.rem(mp + d, nmp)
            send(src_of(peer), got.at[mp], ssem, rsem, {"mp": peer})

    def wait_y(ref, sem):
        wait(ref.at[pl.ds(0, nmp - 1)], sem)

    order = {1: (0,), 2: (1, 0), 4: (2, 1, 3, 0)}[nb4]
    rows1 = (r.mid1, r.land1, r.via1, r.xsem1, r.rsem.at[1], r.rsem.at[2], r.vsem1)
    rows2 = (r.mid2, r.land2, r.via2, r.xsem2, r.rsem2.at[1], r.rsem2.at[2], r.vsem2)

    half = ng * 8
    loads["agents"].wait()
    xt_all = r.agents[...].T
    r.xt[...] = xt_all.reshape(nmp, HEAD, rows)
    xt = r.xt[mp]
    xt2 = split(xt, 0)
    r.xt2[...] = xt2
    spread = lax.broadcasted_iota(jnp.int32, (ng, half), 1) // 8 == lax.broadcasted_iota(
        jnp.int32, (ng, half), 0
    )
    spread = jnp.where(spread, 1.0, 0.0).astype(BF16)
    loads["sends"].wait()
    wide = mb(r.sends[...].astype(F32).astype(BF16), spread)
    own_slot = lax.broadcasted_iota(jnp.int32, (8, half), 1) % 8 == lax.broadcasted_iota(
        jnp.int32, (8, half), 0
    )
    chunk = 256
    for h in range(2):
        line = jnp.sum(jnp.where(own_slot, wide[h * 8 : h * 8 + 8], 0.0), 0, keepdims=True)
        line = line.astype(jnp.int32)
        for c in range(half // chunk):
            row_id = lax.broadcasted_iota(jnp.int32, (rows, chunk), 0)
            hit = row_id == line[:, c * chunk : (c + 1) * chunk]
            r.st[:, pl.ds(h * half + c * chunk, chunk)] = jnp.where(hit, 1.0, 0.0).astype(BF16)
    rows_out = halves(mb(xt2, r.st[...]))
    packed = jnp.concatenate([rows_out[:, :half], rows_out[:, half:]], 0).T
    r.out1[...] = packed.reshape(nz, nxc, 8, LANES)

    loads["w_value_t"].wait()
    r.vt[:HEAD] = mm(r.w_value_t[...], xt_all)
    r.vt[HEAD:] = jnp.ones((HEAD, rows), F32)
    loads["latents"].wait()
    scores = mm(r.latents[...], xt) * scale
    local_top = jnp.max(scores, 1, keepdims=True)
    weights = jnp.exp(scores - local_top)
    r.weights[...] = weights
    part = mt(weights, r.vt[...])
    lane = lax.broadcasted_iota(jnp.int32, part.shape, 1)
    r.give1[...] = jnp.where(lane >= 96, local_top, part).reshape(r.give1.shape)
    pl.semaphore_wait(barrier, nz + nxc + nmp - 3)
    group_start(r.give1, r.got1, r.s1)
    for i in order:
        rows_x(i, r.out1, r.mid1, r.rsem.at[0], r.xsem1)

    loads["degree"].wait()
    loads["neighbours_t"].wait()
    degree = r.degree[...].astype(F32)
    inv_degree = 1.0 / degree
    slot = lax.broadcasted_iota(jnp.int32, (SLOTS, rows), 0)
    near = r.neighbours_t[...]
    far = near - rows
    k = far & 15
    far_col = rows + (k >> 3) * half + (far >> 4) * 8 + (k & 7)
    column = jnp.where(near < rows, near, far_col)
    column = jnp.where(slot < r.degree[...], column, -1)
    r.nbm[...] = column.astype(F32).T.astype(jnp.int32)
    width = rows + 2 * half
    part_width = 768 if width % 768 == 0 else 256

    def count_rows(b):
        row = pl.multiple_of(b * 16, 16)
        nb = r.nbm[pl.ds(row, 16), :]
        for c in range(width // part_width):
            col = lax.broadcasted_iota(jnp.int32, (16, part_width), 1) + c * part_width
            acc = jnp.zeros((16, part_width), F32)
            for s in range(SLOTS):
                acc = acc + jnp.where(nb[:, s : s + 1] == col, 1.0, 0.0)
            r.counts[pl.ds(row, 16), pl.ds(c * part_width, part_width)] = acc.astype(BF16)

    def count_part(p):
        blocks = rows // 64
        loop(p * blocks, (p + 1) * blocks, count_rows)

    wait_x(r.got1, r.s1.at[1])
    r.piece1[...] = merged(r.got1)
    z_share(r.piece1, r.gotz1, r.s1)
    for i in order:
        rows_z(i, *rows1)
    rows_relay(*rows1)
    count_part(0)
    loads["w_local_t"].wait()
    r.wlt[mp] = r.w_local_t[...]
    y_send(lambda peer: r.w_local_t, r.wlt, r.ysem.at[0], r.ysem.at[1])
    count_part(1)
    count_part(2)
    loads["cotangent"].wait()
    loads["w_down"].wait()
    loads["w_up"].wait()
    ct_all = r.cotangent[...].T
    r.ct[...] = ct_all.reshape(nmp, HEAD, rows)
    r.dact[...] = mm(r.w_down[...], ct_all)
    r.wut[...] = r.w_up[...].T
    r.wdt[...] = r.w_down[...].T
    wait_z(r.gotz1, r.s1.at[3])
    r.full1[xc] = merged(r.gotz1)
    group_gather(r.full1, r.s1)
    count_part(3)
    wait_y(r.wlt, r.ysem.at[1])
    wl_t = r.wlt[...].reshape(dim, dim)
    wl = wl_t.T
    r.wl[...] = wl.reshape(nmp, HEAD, dim)
    r.wlu[...] = mm(wl, r.w_up[...])
    r.dmean_ct[...] = mm(r.wl[mp], ct_all)
    own = mbt(xt2, r.counts[:, pl.ds(0, rows)])

    wait_x(r.full1, r.s1.at[5])
    soft = r.full1[...].reshape(VN, LANES)
    inv_total = 1.0 / soft[:, 64:65]
    attended = soft[:, :HEAD] * inv_total
    prob = weights * (jnp.exp(local_top - soft[:, 96:97]) * inv_total)
    r.prob[...] = prob
    r.attended[...] = attended
    fresh = r.latents[...] + attended
    r.fresh[...] = fresh
    a_scores = mm(fresh, xt) * scale
    a_exp = jnp.exp(a_scores - jnp.max(a_scores, 0, keepdims=True))
    a_prob = a_exp / jnp.sum(a_exp, 0, keepdims=True)
    r.aprob[...] = a_prob
    r.fresh_t[...] = fresh.T
    r.read[mp] = mm(r.fresh_t[...], a_prob)
    y_send(lambda peer: r.read.at[mp], r.read, r.ysem.at[2], r.ysem.at[3])

    def put3(row, value):
        r.give3[pl.ds(row, value.shape[0]), :] = value

    blocks = dim // LANES
    units = r.w_up.shape[1]
    base_prob = dim + blocks * units
    weighted_x = mt(prob, xt_all)
    for b in range(blocks):
        put3(base_prob + b * VN, weighted_x[:, b * LANES : (b + 1) * LANES])
    wait_y(r.read, r.ysem.at[3])
    partial_hidden = xt_all + r.read[...].reshape(dim, rows)

    def packed_product(left_low, left_high, land):
        both = split(land[...].reshape(half, LANES), 1)
        low = mb(left_low, both)
        high = mb(left_high, both)
        lane2 = lax.broadcasted_iota(jnp.int32, low.shape, 1) % LANES
        picked = jnp.where(lane2 < HEAD, low, high)
        return (picked[:, :LANES] + picked[:, LANES:]).T

    rows_wait(r.land1, r.rsem.at[2])
    far_sum = packed_product(
        r.counts[:, pl.ds(rows, half)], r.counts[:, pl.ds(rows + half, half)], r.land1
    )
    r.mean[mp] = halves(own + far_sum) * inv_degree
    y_send(lambda peer: r.mean.at[mp], r.mean, r.ysem.at[4], r.ysem.at[5])
    wait_y(r.mean, r.ysem.at[5])

    mean_all = r.mean[...].reshape(dim, rows)
    hid_all = partial_hidden + mm(wl_t, mean_all)
    pre = mm(r.wut[...], hid_all)
    gate = 1.0 / (1.0 + jnp.exp(-pre))
    dpre = r.dact[...] * (gate * (1.0 + pre * (1.0 - gate)))
    r.dhp[...] = mm(r.w_up[...], dpre).reshape(r.dhp.shape)
    y_send(lambda peer: r.dhp.at[peer], r.rdh, r.ysem2.at[2], r.ysem2.at[3])
    r.dmp[...] = mm(r.wlu[...], dpre).reshape(r.dmp.shape)
    y_send(lambda peer: r.dmp.at[peer], r.rdm, r.ysem2.at[0], r.ysem2.at[1])
    act = pre * gate
    r.brp[...] = mm(r.wdt[...], act).reshape(r.brp.shape)
    y_send(lambda peer: r.brp.at[peer], r.rbr, r.ysem2.at[4], r.ysem2.at[5])
    r.rdm[mp] = r.dmp[mp] + r.dmean_ct[...]
    r.rdh[mp] = r.dhp[mp] + r.ct[mp]
    r.hid[...] = hid_all.reshape(r.hid.shape)
    r.rbr[mp] = r.brp[mp] + r.hid[mp]
    put3(0, mt(hid_all, dpre))
    grad_down = mt(act, ct_all)
    for b in range(blocks):
        put3(dim + b * units, grad_down[:, b * LANES : (b + 1) * LANES])
    early = r.give3.shape[0] // nxc

    def piece3(i):
        return pl.ds(pl.multiple_of(i * early, 8), early)

    def start3(d):
        peer = x_peer(d)
        send(
            r.give3.at[piece3(peer)], r.got3.at[xc], r.s3.at[0], r.s3.at[1],
            {"graph": z * nxc + peer},
        )

    loop(1, nxc, start3)
    r.got3[xc] = r.give3[piece3(xc), :]
    wait_y(r.rdh, r.ysem2.at[3])
    dhid = total(r.rdh)

    dprob = mm(r.fresh[...], dhid)
    a_prob = r.aprob[...]
    dagent = a_prob * (dprob - jnp.sum(a_prob * dprob, 0, keepdims=True)) * scale
    dfresh_part = mt(dagent, xt) + mt(a_prob, dhid)
    put_packed(r.give2, dfresh_part)
    group_start(r.give2, r.got2, r.s2)
    grad_local = mt(dhid, mean_all)
    r.give5[...] = jnp.concatenate(
        [grad_local[:, b * LANES : (b + 1) * LANES] for b in range(blocks)], 0
    ).reshape(r.give5.shape)
    group_start(r.give5, r.got5, r.s5)

    wait_y(r.rdm, r.ysem2.at[1])
    dmean = total(r.rdm) * inv_degree
    dtable = halves(mb(split(dmean, 0), r.counts[...]))
    back = jnp.concatenate([dtable[:, rows : rows + half], dtable[:, rows + half :]], 0).T
    r.out2[...] = back.reshape(r.out2.shape)
    for i in order:
        rows_x(i, r.out2, r.mid2, r.rsem2.at[0], r.xsem2)
    wait_x(r.got2, r.s2.at[1])
    r.piece2[...] = total(r.got2)
    z_share(r.piece2, r.gotz2, r.s2)
    wait_x(r.got3, r.s3.at[1])
    tiles_early = early // 8
    tiles_local = r.piece5.shape[0]
    tiles = tiles_early + tiles_local
    r.piece3[...] = total(r.got3).reshape(r.piece3.shape)

    def scatter3(d):
        peer = z_peer(d)

        @pl.when(peer < tiles_early)
        def _():
            send(
                r.piece3.at[peer], r.gotz3.at[z], r.s3.at[2], r.s3.at[3],
                {"graph": peer * nxc + xc},
            )

    loop(1, nz, scatter3)
    owner3 = z < tiles_early
    owner5 = jnp.logical_and(z >= tiles_early, z < tiles)
    owner = z < tiles

    @pl.when(owner3)
    def _():
        r.gotz3[z] = r.piece3[z]

    wait_x(r.got5, r.s5.at[1])
    r.piece5[...] = total(r.got5).reshape(r.piece5.shape)
    for j in range(tiles_local):

        @pl.when(z != tiles_early + j)
        def _():
            send(
                r.piece5.at[j], r.gotz5.at[z], r.s5.at[2 + j], r.s5.at[4],
                {"graph": (tiles_early + j) * nxc + xc},
            )

        @pl.when(z == tiles_early + j)
        def _():
            r.gotz5[z] = r.piece5[j]

    rows_z(order[0], *rows2)
    r.dx[...] = dhid + dtable[:, :rows] + mm(r.fresh_t[...], dagent)
    wait_z(r.gotz2, r.s2.at[3])
    r.full2[xc] = total(r.gotz2)
    group_gather(r.full2, r.s2)

    def gather3(d):
        send(
            r.full3.at[xc, z], r.full3.at[xc, z], r.s3.at[4], r.s3.at[5],
            {"graph": z_peer(d) * nxc + xc},
        )

    @pl.when(owner3)
    def _():
        wait_z(r.gotz3, r.s3.at[3])
        r.full3[xc, z] = total(r.gotz3)
        loop(1, nz, gather3)

    @pl.when(owner5)
    def _():
        wait_z(r.gotz5, r.s5.at[4])
        r.full3[xc, z] = total(r.gotz5)
        loop(1, nz, gather3)

    for i in order[1:2]:
        rows_z(i, *rows2)
    rows_relay(*rows2)

    wait_y(r.rbr, r.ysem2.at[5])
    r.updated_t[...] = total(r.rbr)
    wait_x(r.full2, r.s2.at[5])
    dfresh = get_packed(r.full2)

    dweights = mm(dfresh, r.vt[:HEAD])
    centre = jnp.sum(dfresh * r.attended[...], 1, keepdims=True)
    prob = r.prob[...]
    dscores = prob * (dweights - centre) * scale
    dlatent = mt(dscores, xt)
    put_packed(r.give4, dlatent)
    group_start(r.give4, r.got4, r.s4)
    wait_x(r.got4, r.s4.at[1])
    r.piece4[...] = total(r.got4)
    z_share(r.piece4, r.gotz4, r.s4)
    for i in order[2:]:
        rows_z(i, *rows2)
    dfresh_t = dfresh.T
    dvt = mm(dfresh_t, prob)
    r.dtp[...] = dot(
        r.w_value_t[...], dvt, ((0,), (0,)), lax.Precision.HIGHEST
    ).reshape(r.dtp.shape)
    y_send(lambda peer: r.dtp.at[peer], r.rdt, r.ysem2.at[6], r.ysem2.at[7])
    r.rdt[mp] = r.dtp[mp] + r.dx[...] + mm(r.latents[...].T, dscores)

    wait_z(r.gotz4, r.s4.at[3])
    r.full4[xc] = total(r.gotz4)
    group_gather(r.full4, r.s4)
    @pl.when(owner)
    def _():
        wait(r.full3.at[0, pl.ds(0, tiles - 1)], r.s3.at[5])

    @pl.when(jnp.logical_not(owner))
    def _():
        wait(r.full3.at[0], r.s3.at[5])


    def spread3(d):
        send(
            r.full3.at[xc], r.full3.at[xc], r.s3.at[6], r.s3.at[7],
            {"graph": z * nxc + x_peer(d)},
        )

    loop(1, nxc, spread3)
    wait_y(r.rdt, r.ysem2.at[7])
    dx = total(r.rdt)

    rows_wait(r.land2, r.rsem2.at[2])
    far_back = packed_product(r.st[:, pl.ds(0, half)], r.st[:, pl.ds(half, half)], r.land2)
    r.grad_agents_t[...] = dx + halves(far_back)
    wait_x(r.full4, r.s4.at[5])
    r.grad_latents[...] = (dfresh + get_packed(r.full4)) * factor
    wait_x(r.full3, r.s3.at[7])
    sums3 = r.full3[:, :tiles_early].reshape(r.give3.shape)
    sums5 = r.full3[:, tiles_early:].reshape(blocks * HEAD, LANES)
    r.grad_up[...] = sums3[:dim] * factor
    for b in range(blocks):
        cols = pl.ds(b * LANES, LANES)
        r.grad_down[:, cols] = sums3[dim + b * units : dim + (b + 1) * units] * factor
        r.grad_local_t[:, cols] = sums5[b * HEAD : (b + 1) * HEAD] * factor
        low = base_prob + b * VN
        r.grad_value_t[:, cols] = mm(dfresh_t, sums3[low : low + VN]) * factor

    for give, got_z, full, sems in (
        (r.give1, r.gotz1, r.full1, r.s1),
        (r.give2, r.gotz2, r.full2, r.s2),
        (r.give4, r.gotz4, r.full4, r.s4),
    ):
        wait_x(give, sems.at[0])
        wait_z(got_z, sems.at[2])
        wait_x(full, sems.at[4])
    wait_x(r.got3, r.s3.at[0])
    @pl.when(owner3)
    def _():
        wait(r.piece3.at[pl.ds(0, tiles_early - 1)], r.s3.at[2])

    @pl.when(jnp.logical_not(owner3))
    def _():
        wait(r.piece3, r.s3.at[2])

    for j in range(tiles_local):

        @pl.when(z != tiles_early + j)
        def _():
            wait(r.piece5.at[j], r.s5.at[2 + j])

    @pl.when(owner)
    def _():
        wait_z(r.gotz3, r.s3.at[4])

    wait_x(r.got5, r.s5.at[0])
    wait_x(r.full3, r.s3.at[6])
    for mid, land, sems in ((r.mid1, r.land1, r.rsem), (r.mid2, r.land2, r.rsem2)):
        wait(mid.at[:, pl.ds(0, nxc - 1)], sems.at[0])
        wait(land.at[pl.ds(0, nz - 1)], sems.at[1])
    wait(r.via1, r.vsem1.at[0])
    wait(r.via2, r.vsem2.at[0])
    wait_y(r.wlt, r.ysem.at[0])
    for i, ref in enumerate((r.read, r.mean)):
        wait_y(ref, r.ysem.at[2 + 2 * i])
    for i, ref in enumerate((r.rdm, r.rdh, r.rbr, r.rdt)):
        wait_y(ref, r.ysem2.at[2 * i])


def store(*refs):
    count = len(refs) // 2
    sems = refs[-1]
    copies = [
        pltpu.make_async_copy(refs[i], refs[count + i], sems.at[i]) for i in range(count)
    ]
    for copy in copies:
        copy.start()
    for copy in copies:
        copy.wait()


def on_device(
    nz, agents, latents, w_local, w_value, w_up, w_down, neighbours, degree, send_rows, cotangent
):
    rows, dim = agents.shape
    ng = lax.axis_size("graph")
    nmp = lax.axis_size("mp")
    nxc = ng // nz
    units = w_up.shape[1]
    inputs = dict(
        agents=agents,
        latents=latents,
        w_local_t=w_local.T,
        w_value_t=w_value.T,
        w_up=w_up,
        w_down=w_down,
        neighbours_t=neighbours.T,
        degree=degree.reshape(1, rows),
        sends=send_rows[0].T,
        cotangent=cotangent,
    )
    outs = dict(
        updated_t=(HEAD, rows),
        grad_agents_t=(HEAD, rows),
        grad_latents=(VN, HEAD),
        grad_local_t=(HEAD, dim),
        grad_value_t=(HEAD, dim),
        grad_up=(dim, units),
        grad_down=(units, dim),
    )
    half = ng * 8
    blocks = dim // LANES
    early = (dim + blocks * (units + VN)) // nxc
    local = blocks * HEAD // nxc
    tiles = (early + local) // 8
    rows1 = VN // nxc
    vmem = lambda *shape: pltpu.VMEM(shape, F32)
    dma = lambda n: pltpu.SemaphoreType.DMA((n,))
    scratch = dict(
        xt2=pltpu.VMEM((2 * HEAD, rows), BF16),
        vt=vmem(2 * HEAD, rows),
        st=pltpu.VMEM((rows, 2 * half), BF16),
        counts=pltpu.VMEM((rows, rows + 2 * half), BF16),
        nbm=pltpu.VMEM((rows, SLOTS), jnp.int32),
        weights=vmem(VN, rows),
        prob=vmem(VN, rows),
        aprob=vmem(VN, rows),
        attended=vmem(VN, HEAD),
        fresh=vmem(VN, HEAD),
        fresh_t=vmem(HEAD, VN),
        dact=vmem(units, rows),
        wut=vmem(units, dim),
        wdt=vmem(dim, units),
        wlt=vmem(nmp, HEAD, dim),
        wl=vmem(nmp, HEAD, dim),
        wlu=vmem(dim, units),
        dmean_ct=vmem(HEAD, rows),
        dx=vmem(HEAD, rows),
        xt=vmem(nmp, HEAD, rows),
        ct=vmem(nmp, HEAD, rows),
        read=vmem(nmp, HEAD, rows),
        mean=vmem(nmp, HEAD, rows),
        hid=vmem(nmp, HEAD, rows),
        dmp=vmem(nmp, HEAD, rows),
        rdm=vmem(nmp, HEAD, rows),
        dhp=vmem(nmp, HEAD, rows),
        rdh=vmem(nmp, HEAD, rows),
        brp=vmem(nmp, HEAD, rows),
        rbr=vmem(nmp, HEAD, rows),
        dtp=vmem(nmp, HEAD, rows),
        rdt=vmem(nmp, HEAD, rows),
        give3=vmem(nxc * early, LANES),
        got3=vmem(nxc, early, LANES),
        piece3=vmem(early // 8, 8, LANES),
        piece5=vmem(local // 8, 8, LANES),
        gotz5=vmem(nz, 8, LANES),
        gotz3=vmem(nz, 8, LANES),
        full3=vmem(nxc, tiles, 8, LANES),
        give5=vmem(nxc, local, LANES),
        got5=vmem(nxc, local, LANES),
        s5=dma(5),
        s3=dma(8),
        rsem=dma(3),
        rsem2=dma(3),
        xsem1=dma(4),
        xsem2=dma(4),
        ysem=dma(6),
        ysem2=dma(8),
    )
    for i in (1, 2):
        scratch["out%d" % i] = vmem(nz, nxc, 8, LANES)
        scratch["mid%d" % i] = vmem(nz, nxc, 8, LANES)
        scratch["land%d" % i] = vmem(nz, nxc, 8, LANES)
        scratch["via%d" % i] = vmem(nxc - nxc // 2, 8, LANES)
        scratch["vsem%d" % i] = dma(2)
    for i, n in ((1, rows1), (2, rows1 // 2), (4, rows1 // 2)):
        scratch["give%d" % i] = vmem(nxc, n, LANES)
        scratch["got%d" % i] = vmem(nxc, n, LANES)
        scratch["piece%d" % i] = vmem(n, LANES)
        scratch["gotz%d" % i] = vmem(nz, n, LANES)
        scratch["full%d" % i] = vmem(nxc, n, LANES)
        scratch["s%d" % i] = dma(6)
    for name, value in inputs.items():
        scratch[name] = pltpu.VMEM(value.shape, value.dtype)
    scratch["lsem"] = dma(len(inputs))
    names = [name + "_hbm" for name in inputs] + list(outs) + list(scratch)
    spec = pl.BlockSpec(memory_space=pltpu.VMEM)
    far_spec = pl.BlockSpec(memory_space=pltpu.HBM)
    result = pl.pallas_call(
        functools.partial(layer, nz, nxc, nmp, rows, dim, names, list(inputs)),
        out_shape=[jax.ShapeDtypeStruct(shape, F32) for shape in outs.values()],
        in_specs=[far_spec] * len(inputs),
        out_specs=[spec] * len(outs),
        scratch_shapes=list(scratch.values()),
        compiler_params=pltpu.CompilerParams(
            collective_id=0, has_side_effects=True, vmem_limit_bytes=62_000_000
        ),
        name="layer",
    )(*inputs.values())
    result = pl.pallas_call(
        store,
        out_shape=[jax.ShapeDtypeStruct(shape, F32) for shape in outs.values()],
        in_specs=[spec] * len(outs),
        out_specs=[far_spec] * len(outs),
        scratch_shapes=[dma(len(outs))],
        compiler_params=pltpu.CompilerParams(vmem_limit_bytes=62_000_000),
        name="store",
    )(*result)
    updated, grad_agents, grad_latents, grad_local, grad_value, grad_up, grad_down = result
    return (
        updated.T,
        grad_agents.T,
        grad_latents,
        grad_local.T,
        grad_value.T,
        grad_up,
        grad_down,
    )


def solution(mesh, nz=16):
    return jax.shard_map(
        functools.partial(on_device, nz),
        mesh=mesh,
        in_specs=(
            P("graph", None),
            P(None, "mp"),
            P(None, "mp"),
            P(None, "mp"),
            P(None, "mp"),
            P("mp", None),
            P("graph", None),
            P("graph"),
            P("graph", None, None),
            P("graph", None),
        ),
        out_specs=(
            P("graph", "mp"),
            P("graph", "mp"),
            P(None, "mp"),
            P(None, "mp"),
            P(None, "mp"),
            P(None, "mp"),
            P("mp", None),
        ),
        check_vma=False,
    )
```

```python
import functools
import math
from types import SimpleNamespace

import jax
import jax.numpy as jnp
from jax import lax
from jax.experimental import pallas as pl
from jax.experimental.pallas import tpu as pltpu
from jax.sharding import PartitionSpec as P

HEAD = 64
VN = 64
SLOTS = 16
LANES = 128
MESH = pl.DeviceIdType.MESH
F32 = jnp.float32
BF16 = jnp.bfloat16


def dot(left, right, contract, precision):
    return lax.dot_general(
        left, right, (contract, ((), ())), precision=precision, preferred_element_type=F32
    )


def mm(left, right):
    return dot(left, right, ((1,), (0,)), lax.Precision.HIGHEST)


def mt(left, right):
    return dot(left, right, ((1,), (1,)), lax.Precision.HIGHEST)


def mb(left, right):
    return dot(left, right, ((1,), (0,)), lax.Precision.DEFAULT)


def mbt(left, right):
    return dot(left, right, ((1,), (1,)), lax.Precision.DEFAULT)


def split(x, axis):
    high = x.astype(BF16)
    low = (x - high.astype(F32)).astype(BF16)
    return jnp.concatenate([high, low], axis)


def halves(x):
    half = x.shape[0] // 2
    return x[:half] + x[half:]


def layer(nz, nxc, nmp, rows, dim, names, given, *refs):
    r = SimpleNamespace(**dict(zip(names, refs)))
    loads = {
        name: pltpu.make_async_copy(getattr(r, name + "_hbm"), getattr(r, name), r.lsem.at[i])
        for i, name in enumerate(given)
    }
    for load in loads.values():
        load.start()
    graph = lax.axis_index("graph")
    mp = lax.axis_index("mp")
    z = graph // nxc
    xc = lax.rem(graph, nxc)
    nb4 = nz // 4
    zb = z // 4
    zm = lax.rem(z, 4)
    ng = nz * nxc
    scale = 1.0 / math.sqrt(HEAD)
    factor = 1.0 / math.sqrt(rows * ng)

    def z_peer(d):
        return lax.rem(z + d, nz)

    def x_peer(d):
        return lax.rem(xc + d, nxc)

    def send(src, dst, ssem, rsem, device):
        pltpu.make_async_remote_copy(
            src_ref=src,
            dst_ref=dst,
            send_sem=ssem,
            recv_sem=rsem,
            device_id=device,
            device_id_type=MESH,
        ).start()

    def wait(ref, sem):
        pltpu.make_async_copy(ref, ref, sem).wait()

    def loop(low, high, body):
        def step(d, carry):
            body(d)
            return carry

        lax.fori_loop(low, high, step, 0)

    barrier = pltpu.get_barrier_semaphore()

    def greet(device):
        pl.semaphore_signal(barrier, inc=1, device_id=device, device_id_type=MESH)

    loop(1, nz, lambda d: greet({"graph": z_peer(d) * nxc + xc}))
    loop(1, nxc, lambda d: greet({"graph": z * nxc + x_peer(d)}))
    loop(1, nmp, lambda d: greet({"mp": lax.rem(mp + d, nmp)}))

    def group_start(give, got, sems):
        def go(d):
            peer = x_peer(d)
            send(give.at[peer], got.at[xc], sems.at[0], sems.at[1], {"graph": z * nxc + peer})

        loop(1, nxc, go)
        got[xc] = give[xc]

    def z_share(piece, got, sems):
        def go(d):
            send(piece, got.at[z], sems.at[2], sems.at[3], {"graph": z_peer(d) * nxc + xc})

        loop(1, nz, go)
        got[z] = piece[...]

    def group_gather(full, sems):
        def go(d):
            send(full.at[xc], full.at[xc], sems.at[4], sems.at[5], {"graph": z * nxc + x_peer(d)})

        loop(1, nxc, go)

    def wait_x(ref, sem):
        wait(ref.at[pl.ds(0, nxc - 1)], sem)

    def wait_z(ref, sem):
        wait(ref.at[pl.ds(0, nz - 1)], sem)

    def put_packed(ref, value):
        packed = jnp.concatenate([value[: VN // 2], value[VN // 2 :]], 1)
        n = ref.shape[1]
        for i in range(ref.shape[0]):
            ref[i] = packed[i * n : (i + 1) * n]

    def get_packed(ref):
        packed = jnp.concatenate([ref[i] for i in range(ref.shape[0])], 0)
        return jnp.concatenate([packed[:, :HEAD], packed[:, HEAD:]], 0)

    def total(ref):
        acc = ref[0]
        for i in range(1, ref.shape[0]):
            acc = acc + ref[i]
        return acc

    def merged(ref):
        count = ref.shape[0]
        parts = [ref[i] for i in range(count)]
        tops = [part[:, 96:97] for part in parts]
        top = functools.reduce(jnp.maximum, tops)
        acc = parts[0] * jnp.exp(tops[0] - top)
        for i in range(1, count):
            acc = acc + parts[i] * jnp.exp(tops[i] - top)
        lane = lax.broadcasted_iota(jnp.int32, acc.shape, 1)
        return jnp.where(lane >= 96, top, acc)

    def rows_x(i, out, mid, xs, xr):
        base = lax.rem(zb + nb4 - i, nb4) * 4

        def go(d):
            peer = x_peer(d)
            send(
                out.at[pl.ds(base, 4), peer],
                mid.at[pl.ds(base, 4), xc],
                xs,
                xr.at[i],
                {"graph": z * nxc + peer},
            )

        loop(1, nxc, go)
        mid[pl.ds(base, 4), xc] = out[pl.ds(base, 4), xc]

    def rows_z(i, mid, land, via, xr, zs, zr, rs):
        base = lax.rem(zb + nb4 - i, nb4) * 4
        wait(mid.at[pl.ds(0, 4), pl.ds(0, nxc - 1)], xr.at[i])
        for d in range(1 if i == 0 else 0, 4):
            peer = base + lax.rem(zm + d, 4)
            device = {"graph": peer * nxc + xc}
            if i == nb4 // 2 and d == 0:
                send(mid.at[peer, upper], via, rs.at[0], rs.at[1], {"graph": z_peer(nz - 1) * nxc + xc})
                send(mid.at[peer, lower], land.at[z, lower], zs, zr, device)
            else:
                send(mid.at[peer], land.at[z], zs, zr, device)
        if i == 0:
            land[z] = mid[z]

    lower = pl.ds(0, nxc // 2)
    upper = pl.ds(nxc // 2, nxc - nxc // 2)

    def rows_relay(mid, land, via, xr, zs, zr, rs):
        wait(via, rs.at[1])
        send(
            via, land.at[z_peer(1), upper], zs, zr,
            {"graph": z_peer(nz // 2 + 1) * nxc + xc},
        )

    def rows_wait(land, zr):
        wait(land.at[pl.ds(0, nz - 1)], zr)

    def y_send(src_of, got, ssem, rsem):
        for d in range(1, nmp):
            peer = lax.rem(mp + d, nmp)
            send(src_of(peer), got.at[mp], ssem, rsem, {"mp": peer})

    def wait_y(ref, sem):
        wait(ref.at[pl.ds(0, nmp - 1)], sem)

    order = {1: (0,), 2: (1, 0), 4: (2, 1, 3, 0)}[nb4]
    rows1 = (r.mid1, r.land1, r.via1, r.xsem1, r.rsem.at[1], r.rsem.at[2], r.vsem1)
    rows2 = (r.mid2, r.land2, r.via2, r.xsem2, r.rsem2.at[1], r.rsem2.at[2], r.vsem2)

    half = ng * 8
    loads["agents"].wait()
    xt_all = r.agents[...].T
    r.xt[...] = xt_all.reshape(nmp, HEAD, rows)
    xt = r.xt[mp]
    xt2 = split(xt, 0)
    r.xt2[...] = xt2
    spread = lax.broadcasted_iota(jnp.int32, (ng, half), 1) // 8 == lax.broadcasted_iota(
        jnp.int32, (ng, half), 0
    )
    spread = jnp.where(spread, 1.0, 0.0).astype(BF16)
    loads["sends"].wait()
    wide = mb(r.sends[...].astype(F32).astype(BF16), spread)
    own_slot = lax.broadcasted_iota(jnp.int32, (8, half), 1) % 8 == lax.broadcasted_iota(
        jnp.int32, (8, half), 0
    )
    chunk = 256
    for h in range(2):
        line = jnp.sum(jnp.where(own_slot, wide[h * 8 : h * 8 + 8], 0.0), 0, keepdims=True)
        line = line.astype(jnp.int32)
        for c in range(half // chunk):
            row_id = lax.broadcasted_iota(jnp.int32, (rows, chunk), 0)
            hit = row_id == line[:, c * chunk : (c + 1) * chunk]
            r.st[:, pl.ds(h * half + c * chunk, chunk)] = jnp.where(hit, 1.0, 0.0).astype(BF16)
    rows_out = halves(mb(xt2, r.st[...]))
    packed = jnp.concatenate([rows_out[:, :half], rows_out[:, half:]], 0).T
    r.out1[...] = packed.reshape(nz, nxc, 8, LANES)

    loads["w_value_t"].wait()
    r.vt[:HEAD] = mm(r.w_value_t[...], xt_all)
    r.vt[HEAD:] = jnp.ones((HEAD, rows), F32)
    loads["latents"].wait()
    scores = mm(r.latents[...], xt) * scale
    local_top = jnp.max(scores, 1, keepdims=True)
    weights = jnp.exp(scores - local_top)
    r.weights[...] = weights
    part = mt(weights, r.vt[...])
    lane = lax.broadcasted_iota(jnp.int32, part.shape, 1)
    r.give1[...] = jnp.where(lane >= 96, local_top, part).reshape(r.give1.shape)
    pl.semaphore_wait(barrier, nz + nxc + nmp - 3)
    group_start(r.give1, r.got1, r.s1)
    for i in order:
        rows_x(i, r.out1, r.mid1, r.rsem.at[0], r.xsem1)

    loads["degree"].wait()
    loads["neighbours_t"].wait()
    degree = r.degree[...].astype(F32)
    inv_degree = 1.0 / degree
    slot = lax.broadcasted_iota(jnp.int32, (SLOTS, rows), 0)
    near = r.neighbours_t[...]
    far = near - rows
    k = far & 15
    far_col = rows + (k >> 3) * half + (far >> 4) * 8 + (k & 7)
    column = jnp.where(near < rows, near, far_col)
    column = jnp.where(slot < r.degree[...], column, -1)
    r.nbm[...] = column.astype(F32).T.astype(jnp.int32)
    width = rows + 2 * half
    part_width = 768 if width % 768 == 0 else 256

    def count_rows(b):
        row = pl.multiple_of(b * 16, 16)
        nb = r.nbm[pl.ds(row, 16), :]
        for c in range(width // part_width):
            col = lax.broadcasted_iota(jnp.int32, (16, part_width), 1) + c * part_width
            acc = jnp.zeros((16, part_width), F32)
            for s in range(SLOTS):
                acc = acc + jnp.where(nb[:, s : s + 1] == col, 1.0, 0.0)
            r.counts[pl.ds(row, 16), pl.ds(c * part_width, part_width)] = acc.astype(BF16)

    def count_part(p):
        blocks = rows // 64
        loop(p * blocks, (p + 1) * blocks, count_rows)

    wait_x(r.got1, r.s1.at[1])
    r.piece1[...] = merged(r.got1)
    z_share(r.piece1, r.gotz1, r.s1)
    for i in order:
        rows_z(i, *rows1)
    rows_relay(*rows1)
    count_part(0)
    loads["w_local_t"].wait()
    r.wlt[mp] = r.w_local_t[...]
    y_send(lambda peer: r.w_local_t, r.wlt, r.ysem.at[0], r.ysem.at[1])
    count_part(1)
    count_part(2)
    loads["cotangent"].wait()
    loads["w_down"].wait()
    loads["w_up"].wait()
    ct_all = r.cotangent[...].T
    r.ct[...] = ct_all.reshape(nmp, HEAD, rows)
    r.dact[...] = mm(r.w_down[...], ct_all)
    r.wut[...] = r.w_up[...].T
    r.wdt[...] = r.w_down[...].T
    wait_z(r.gotz1, r.s1.at[3])
    r.full1[xc] = merged(r.gotz1)
    group_gather(r.full1, r.s1)
    count_part(3)
    wait_y(r.wlt, r.ysem.at[1])
    wl_t = r.wlt[...].reshape(dim, dim)
    wl = wl_t.T
    r.wl[...] = wl.reshape(nmp, HEAD, dim)
    r.wlu[...] = mm(wl, r.w_up[...])
    r.dmean_ct[...] = mm(r.wl[mp], ct_all)
    own = mbt(xt2, r.counts[:, pl.ds(0, rows)])

    wait_x(r.full1, r.s1.at[5])
    soft = r.full1[...].reshape(VN, LANES)
    inv_total = 1.0 / soft[:, 64:65]
    attended = soft[:, :HEAD] * inv_total
    prob = weights * (jnp.exp(local_top - soft[:, 96:97]) * inv_total)
    r.prob[...] = prob
    r.attended[...] = attended
    fresh = r.latents[...] + attended
    r.fresh[...] = fresh
    a_scores = mm(fresh, xt) * scale
    a_exp = jnp.exp(a_scores - jnp.max(a_scores, 0, keepdims=True))
    a_prob = a_exp / jnp.sum(a_exp, 0, keepdims=True)
    r.aprob[...] = a_prob
    r.fresh_t[...] = fresh.T
    r.read[mp] = mm(r.fresh_t[...], a_prob)
    y_send(lambda peer: r.read.at[mp], r.read, r.ysem.at[2], r.ysem.at[3])

    def put3(row, value):
        r.give3[pl.ds(row, value.shape[0]), :] = value

    blocks = dim // LANES
    units = r.w_up.shape[1]
    base_prob = dim + blocks * units
    weighted_x = mt(prob, xt_all)
    for b in range(blocks):
        put3(base_prob + b * VN, weighted_x[:, b * LANES : (b + 1) * LANES])
    wait_y(r.read, r.ysem.at[3])
    partial_hidden = xt_all + r.read[...].reshape(dim, rows)

    def packed_product(left_low, left_high, land):
        both = split(land[...].reshape(half, LANES), 1)
        low = mb(left_low, both)
        high = mb(left_high, both)
        lane2 = lax.broadcasted_iota(jnp.int32, low.shape, 1) % LANES
        picked = jnp.where(lane2 < HEAD, low, high)
        return (picked[:, :LANES] + picked[:, LANES:]).T

    rows_wait(r.land1, r.rsem.at[2])
    far_sum = packed_product(
        r.counts[:, pl.ds(rows, half)], r.counts[:, pl.ds(rows + half, half)], r.land1
    )
    r.mean[mp] = halves(own + far_sum) * inv_degree
    y_send(lambda peer: r.mean.at[mp], r.mean, r.ysem.at[4], r.ysem.at[5])
    wait_y(r.mean, r.ysem.at[5])

    mean_all = r.mean[...].reshape(dim, rows)
    hid_all = partial_hidden + mm(wl_t, mean_all)
    pre = mm(r.wut[...], hid_all)
    gate = 1.0 / (1.0 + jnp.exp(-pre))
    dpre = r.dact[...] * (gate * (1.0 + pre * (1.0 - gate)))
    r.dhp[...] = mm(r.w_up[...], dpre).reshape(r.dhp.shape)
    y_send(lambda peer: r.dhp.at[peer], r.rdh, r.ysem2.at[2], r.ysem2.at[3])
    r.dmp[...] = mm(r.wlu[...], dpre).reshape(r.dmp.shape)
    y_send(lambda peer: r.dmp.at[peer], r.rdm, r.ysem2.at[0], r.ysem2.at[1])
    act = pre * gate
    r.brp[...] = mm(r.wdt[...], act).reshape(r.brp.shape)
    y_send(lambda peer: r.brp.at[peer], r.rbr, r.ysem2.at[4], r.ysem2.at[5])
    r.rdm[mp] = r.dmp[mp] + r.dmean_ct[...]
    r.rdh[mp] = r.dhp[mp] + r.ct[mp]
    r.hid[...] = hid_all.reshape(r.hid.shape)
    r.rbr[mp] = r.brp[mp] + r.hid[mp]
    put3(0, mt(hid_all, dpre))
    grad_down = mt(act, ct_all)
    for b in range(blocks):
        put3(dim + b * units, grad_down[:, b * LANES : (b + 1) * LANES])
    early = r.give3.shape[0] // nxc

    def piece3(i):
        return pl.ds(pl.multiple_of(i * early, 8), early)

    def start3(d):
        peer = x_peer(d)
        send(
            r.give3.at[piece3(peer)], r.got3.at[xc], r.s3.at[0], r.s3.at[1],
            {"graph": z * nxc + peer},
        )

    loop(1, nxc, start3)
    r.got3[xc] = r.give3[piece3(xc), :]
    wait_y(r.rdh, r.ysem2.at[3])
    dhid = total(r.rdh)

    dprob = mm(r.fresh[...], dhid)
    a_prob = r.aprob[...]
    dagent = a_prob * (dprob - jnp.sum(a_prob * dprob, 0, keepdims=True)) * scale
    dfresh_part = mt(dagent, xt) + mt(a_prob, dhid)
    put_packed(r.give2, dfresh_part)
    group_start(r.give2, r.got2, r.s2)
    grad_local = mt(dhid, mean_all)
    r.give5[...] = jnp.concatenate(
        [grad_local[:, b * LANES : (b + 1) * LANES] for b in range(blocks)], 0
    ).reshape(r.give5.shape)
    group_start(r.give5, r.got5, r.s5)

    wait_y(r.rdm, r.ysem2.at[1])
    dmean = total(r.rdm) * inv_degree
    dtable = halves(mb(split(dmean, 0), r.counts[...]))
    back = jnp.concatenate([dtable[:, rows : rows + half], dtable[:, rows + half :]], 0).T
    r.out2[...] = back.reshape(r.out2.shape)
    for i in order:
        rows_x(i, r.out2, r.mid2, r.rsem2.at[0], r.xsem2)
    wait_x(r.got2, r.s2.at[1])
    r.piece2[...] = total(r.got2)
    z_share(r.piece2, r.gotz2, r.s2)
    wait_x(r.got3, r.s3.at[1])
    tiles_early = early // 8
    tiles_local = r.piece5.shape[0]
    tiles = tiles_early + tiles_local
    r.piece3[...] = total(r.got3).reshape(r.piece3.shape)

    def scatter3(d):
        peer = z_peer(d)

        @pl.when(peer < tiles_early)
        def _():
            send(
                r.piece3.at[peer], r.gotz3.at[z], r.s3.at[2], r.s3.at[3],
                {"graph": peer * nxc + xc},
            )

    loop(1, nz, scatter3)
    owner3 = z < tiles_early
    owner5 = jnp.logical_and(z >= tiles_early, z < tiles)
    owner = z < tiles

    @pl.when(owner3)
    def _():
        r.gotz3[z] = r.piece3[z]

    wait_x(r.got5, r.s5.at[1])
    r.piece5[...] = total(r.got5).reshape(r.piece5.shape)
    for j in range(tiles_local):

        @pl.when(z != tiles_early + j)
        def _():
            send(
                r.piece5.at[j], r.gotz5.at[z], r.s5.at[2 + j], r.s5.at[4],
                {"graph": (tiles_early + j) * nxc + xc},
            )

        @pl.when(z == tiles_early + j)
        def _():
            r.gotz5[z] = r.piece5[j]

    rows_z(order[0], *rows2)
    r.dx[...] = dhid + dtable[:, :rows] + mm(r.fresh_t[...], dagent)
    wait_z(r.gotz2, r.s2.at[3])
    r.full2[xc] = total(r.gotz2)
    group_gather(r.full2, r.s2)

    def gather3(d):
        send(
            r.full3.at[xc, z], r.full3.at[xc, z], r.s3.at[4], r.s3.at[5],
            {"graph": z_peer(d) * nxc + xc},
        )

    @pl.when(owner3)
    def _():
        wait_z(r.gotz3, r.s3.at[3])
        r.full3[xc, z] = total(r.gotz3)
        loop(1, nz, gather3)

    @pl.when(owner5)
    def _():
        wait_z(r.gotz5, r.s5.at[4])
        r.full3[xc, z] = total(r.gotz5)
        loop(1, nz, gather3)

    for i in order[1:2]:
        rows_z(i, *rows2)
    rows_relay(*rows2)

    wait_y(r.rbr, r.ysem2.at[5])
    r.updated_t[...] = total(r.rbr)
    wait_x(r.full2, r.s2.at[5])
    dfresh = get_packed(r.full2)

    dweights = mm(dfresh, r.vt[:HEAD])
    centre = jnp.sum(dfresh * r.attended[...], 1, keepdims=True)
    prob = r.prob[...]
    dscores = prob * (dweights - centre) * scale
    dlatent = mt(dscores, xt)
    put_packed(r.give4, dlatent)
    group_start(r.give4, r.got4, r.s4)
    wait_x(r.got4, r.s4.at[1])
    r.piece4[...] = total(r.got4)
    z_share(r.piece4, r.gotz4, r.s4)
    for i in order[2:]:
        rows_z(i, *rows2)
    dfresh_t = dfresh.T
    dvt = mm(dfresh_t, prob)
    r.dtp[...] = dot(
        r.w_value_t[...], dvt, ((0,), (0,)), lax.Precision.HIGHEST
    ).reshape(r.dtp.shape)
    y_send(lambda peer: r.dtp.at[peer], r.rdt, r.ysem2.at[6], r.ysem2.at[7])
    r.rdt[mp] = r.dtp[mp] + r.dx[...] + mm(r.latents[...].T, dscores)

    @pl.when(owner)
    def _():
        wait(r.full3.at[0, pl.ds(0, tiles - 1)], r.s3.at[5])

    @pl.when(jnp.logical_not(owner))
    def _():
        wait(r.full3.at[0], r.s3.at[5])


    def spread3(d):
        send(
            r.full3.at[xc], r.full3.at[xc], r.s3.at[6], r.s3.at[7],
            {"graph": z * nxc + x_peer(d)},
        )

    loop(1, nxc, spread3)
    wait_z(r.gotz4, r.s4.at[3])
    r.full4[xc] = total(r.gotz4)
    group_gather(r.full4, r.s4)
    wait_y(r.rdt, r.ysem2.at[7])
    dx = total(r.rdt)

    rows_wait(r.land2, r.rsem2.at[2])
    far_back = packed_product(r.st[:, pl.ds(0, half)], r.st[:, pl.ds(half, half)], r.land2)
    r.grad_agents_t[...] = dx + halves(far_back)
    wait_x(r.full4, r.s4.at[5])
    r.grad_latents[...] = (dfresh + get_packed(r.full4)) * factor
    wait_x(r.full3, r.s3.at[7])
    sums3 = r.full3[:, :tiles_early].reshape(r.give3.shape)
    sums5 = r.full3[:, tiles_early:].reshape(blocks * HEAD, LANES)
    r.grad_up[...] = sums3[:dim] * factor
    for b in range(blocks):
        cols = pl.ds(b * LANES, LANES)
        r.grad_down[:, cols] = sums3[dim + b * units : dim + (b + 1) * units] * factor
        r.grad_local_t[:, cols] = sums5[b * HEAD : (b + 1) * HEAD] * factor
        low = base_prob + b * VN
        r.grad_value_t[:, cols] = mm(dfresh_t, sums3[low : low + VN]) * factor

    for give, got_z, full, sems in (
        (r.give1, r.gotz1, r.full1, r.s1),
        (r.give2, r.gotz2, r.full2, r.s2),
        (r.give4, r.gotz4, r.full4, r.s4),
    ):
        wait_x(give, sems.at[0])
        wait_z(got_z, sems.at[2])
        wait_x(full, sems.at[4])
    wait_x(r.got3, r.s3.at[0])
    @pl.when(owner3)
    def _():
        wait(r.piece3.at[pl.ds(0, tiles_early - 1)], r.s3.at[2])

    @pl.when(jnp.logical_not(owner3))
    def _():
        wait(r.piece3, r.s3.at[2])

    for j in range(tiles_local):

        @pl.when(z != tiles_early + j)
        def _():
            wait(r.piece5.at[j], r.s5.at[2 + j])

    @pl.when(owner)
    def _():
        wait_z(r.gotz3, r.s3.at[4])

    wait_x(r.got5, r.s5.at[0])
    wait_x(r.full3, r.s3.at[6])
    for mid, land, sems in ((r.mid1, r.land1, r.rsem), (r.mid2, r.land2, r.rsem2)):
        wait(mid.at[:, pl.ds(0, nxc - 1)], sems.at[0])
        wait(land.at[pl.ds(0, nz - 1)], sems.at[1])
    wait(r.via1, r.vsem1.at[0])
    wait(r.via2, r.vsem2.at[0])
    wait_y(r.wlt, r.ysem.at[0])
    for i, ref in enumerate((r.read, r.mean)):
        wait_y(ref, r.ysem.at[2 + 2 * i])
    for i, ref in enumerate((r.rdm, r.rdh, r.rbr, r.rdt)):
        wait_y(ref, r.ysem2.at[2 * i])


def store(*refs):
    count = len(refs) // 2
    sems = refs[-1]
    copies = [
        pltpu.make_async_copy(refs[i], refs[count + i], sems.at[i]) for i in range(count)
    ]
    for copy in copies:
        copy.start()
    for copy in copies:
        copy.wait()


def on_device(
    nz, agents, latents, w_local, w_value, w_up, w_down, neighbours, degree, send_rows, cotangent
):
    rows, dim = agents.shape
    ng = lax.axis_size("graph")
    nmp = lax.axis_size("mp")
    nxc = ng // nz
    units = w_up.shape[1]
    inputs = dict(
        agents=agents,
        latents=latents,
        w_local_t=w_local.T,
        w_value_t=w_value.T,
        w_up=w_up,
        w_down=w_down,
        neighbours_t=neighbours.T,
        degree=degree.reshape(1, rows),
        sends=send_rows[0].T,
        cotangent=cotangent,
    )
    outs = dict(
        updated_t=(HEAD, rows),
        grad_agents_t=(HEAD, rows),
        grad_latents=(VN, HEAD),
        grad_local_t=(HEAD, dim),
        grad_value_t=(HEAD, dim),
        grad_up=(dim, units),
        grad_down=(units, dim),
    )
    half = ng * 8
    blocks = dim // LANES
    early = (dim + blocks * (units + VN)) // nxc
    local = blocks * HEAD // nxc
    tiles = (early + local) // 8
    rows1 = VN // nxc
    vmem = lambda *shape: pltpu.VMEM(shape, F32)
    dma = lambda n: pltpu.SemaphoreType.DMA((n,))
    scratch = dict(
        xt2=pltpu.VMEM((2 * HEAD, rows), BF16),
        vt=vmem(2 * HEAD, rows),
        st=pltpu.VMEM((rows, 2 * half), BF16),
        counts=pltpu.VMEM((rows, rows + 2 * half), BF16),
        nbm=pltpu.VMEM((rows, SLOTS), jnp.int32),
        weights=vmem(VN, rows),
        prob=vmem(VN, rows),
        aprob=vmem(VN, rows),
        attended=vmem(VN, HEAD),
        fresh=vmem(VN, HEAD),
        fresh_t=vmem(HEAD, VN),
        dact=vmem(units, rows),
        wut=vmem(units, dim),
        wdt=vmem(dim, units),
        wlt=vmem(nmp, HEAD, dim),
        wl=vmem(nmp, HEAD, dim),
        wlu=vmem(dim, units),
        dmean_ct=vmem(HEAD, rows),
        dx=vmem(HEAD, rows),
        xt=vmem(nmp, HEAD, rows),
        ct=vmem(nmp, HEAD, rows),
        read=vmem(nmp, HEAD, rows),
        mean=vmem(nmp, HEAD, rows),
        hid=vmem(nmp, HEAD, rows),
        dmp=vmem(nmp, HEAD, rows),
        rdm=vmem(nmp, HEAD, rows),
        dhp=vmem(nmp, HEAD, rows),
        rdh=vmem(nmp, HEAD, rows),
        brp=vmem(nmp, HEAD, rows),
        rbr=vmem(nmp, HEAD, rows),
        dtp=vmem(nmp, HEAD, rows),
        rdt=vmem(nmp, HEAD, rows),
        give3=vmem(nxc * early, LANES),
        got3=vmem(nxc, early, LANES),
        piece3=vmem(early // 8, 8, LANES),
        piece5=vmem(local // 8, 8, LANES),
        gotz5=vmem(nz, 8, LANES),
        gotz3=vmem(nz, 8, LANES),
        full3=vmem(nxc, tiles, 8, LANES),
        give5=vmem(nxc, local, LANES),
        got5=vmem(nxc, local, LANES),
        s5=dma(5),
        s3=dma(8),
        rsem=dma(3),
        rsem2=dma(3),
        xsem1=dma(4),
        xsem2=dma(4),
        ysem=dma(6),
        ysem2=dma(8),
    )
    for i in (1, 2):
        scratch["out%d" % i] = vmem(nz, nxc, 8, LANES)
        scratch["mid%d" % i] = vmem(nz, nxc, 8, LANES)
        scratch["land%d" % i] = vmem(nz, nxc, 8, LANES)
        scratch["via%d" % i] = vmem(nxc - nxc // 2, 8, LANES)
        scratch["vsem%d" % i] = dma(2)
    for i, n in ((1, rows1), (2, rows1 // 2), (4, rows1 // 2)):
        scratch["give%d" % i] = vmem(nxc, n, LANES)
        scratch["got%d" % i] = vmem(nxc, n, LANES)
        scratch["piece%d" % i] = vmem(n, LANES)
        scratch["gotz%d" % i] = vmem(nz, n, LANES)
        scratch["full%d" % i] = vmem(nxc, n, LANES)
        scratch["s%d" % i] = dma(6)
    for name, value in inputs.items():
        scratch[name] = pltpu.VMEM(value.shape, value.dtype)
    scratch["lsem"] = dma(len(inputs))
    names = [name + "_hbm" for name in inputs] + list(outs) + list(scratch)
    spec = pl.BlockSpec(memory_space=pltpu.VMEM)
    far_spec = pl.BlockSpec(memory_space=pltpu.HBM)
    result = pl.pallas_call(
        functools.partial(layer, nz, nxc, nmp, rows, dim, names, list(inputs)),
        out_shape=[jax.ShapeDtypeStruct(shape, F32) for shape in outs.values()],
        in_specs=[far_spec] * len(inputs),
        out_specs=[spec] * len(outs),
        scratch_shapes=list(scratch.values()),
        compiler_params=pltpu.CompilerParams(
            collective_id=0, has_side_effects=True, vmem_limit_bytes=62_000_000
        ),
        name="layer",
    )(*inputs.values())
    result = pl.pallas_call(
        store,
        out_shape=[jax.ShapeDtypeStruct(shape, F32) for shape in outs.values()],
        in_specs=[spec] * len(outs),
        out_specs=[far_spec] * len(outs),
        scratch_shapes=[dma(len(outs))],
        compiler_params=pltpu.CompilerParams(vmem_limit_bytes=62_000_000),
        name="store",
    )(*result)
    updated, grad_agents, grad_latents, grad_local, grad_value, grad_up, grad_down = result
    return (
        updated.T,
        grad_agents.T,
        grad_latents,
        grad_local.T,
        grad_value.T,
        grad_up,
        grad_down,
    )


def solution(mesh, nz=16):
    return jax.shard_map(
        functools.partial(on_device, nz),
        mesh=mesh,
        in_specs=(
            P("graph", None),
            P(None, "mp"),
            P(None, "mp"),
            P(None, "mp"),
            P(None, "mp"),
            P("mp", None),
            P("graph", None),
            P("graph"),
            P("graph", None, None),
            P("graph", None),
        ),
        out_specs=(
            P("graph", "mp"),
            P("graph", "mp"),
            P(None, "mp"),
            P(None, "mp"),
            P(None, "mp"),
            P(None, "mp"),
            P("mp", None),
        ),
        check_vma=False,
    )
```
